512 devices in a mesh: row: 8 (over x, core), col: 16 (over z), depth: 4 (over y).
Axes of the slice: x: 4, y: 4, z: 16, core: 2. Of those that a mesh axis runs over, the one named last changes fastest.
Arguments:
- density: float32 [4096, 4096], P('row', 'col'), as said below
- pattern: int32 [32, 32], P('row', 'col'), may hold values from 0 to 1, as said below
- branch: int32 [4], replicated, may hold values from 0 to 1, as said below
Outputs:
- purified: float32 [4096, 4096], P('row', 'col')
The draws below stay inside these ranges and needn't reach their ends.
Inputs may be any that keep to these rules, and one draw needn't show every extreme that they name: `branch`: each entry is 0 or 1; both values occur. Each entry is 0 or 1, and pattern[i, j] = pattern[j, i]. density is symmetric: density[i, j] = density[j, i].
All inputs are finite; a program needn't handle non-finite values.
Results may differ from the reference program's by a relative error of at most 0.00026.
Values sent between devices are 32-bit elements; how exact they have to be, the bound alone decides.
No kernel may reach another device: no remote copies, remote signals or barrier semaphores. Data moves between devices by JAX's collectives and lax.ppermute only.
A program may use at most 64 MiB of HBM per device.

```python
import jax
import jax.numpy as jnp
from jax import lax

TILE = 128
NB = 32
STEPS = 4
ORDER = 4096


def draw_density(key, part):
    key = jax.random.fold_in(key, 7)
    key_off, key_diag = jax.random.split(key)
    spread = 0.1 / jnp.sqrt(ORDER / 3.0)
    raw_part = jax.random.normal(key_off, (ORDER, ORDER), jnp.float32)
    diag_vals = jax.random.uniform(key_diag, (ORDER,), jnp.float32, 0.3, 0.7)
    off_diag = (raw_part + raw_part.T) * (spread / jnp.sqrt(2.0))
    return off_diag + jnp.diag(diag_vals)


def draw_pattern(key, part):
    key = jax.random.fold_in(key, 11)
    picks = jax.random.randint(key, (NB, NB), 0, 3)
    chosen = jnp.where(picks == 0, 1, 0).astype(jnp.int32)
    row_ids = lax.broadcasted_iota(jnp.int32, (NB, NB), 0)
    col_ids = lax.broadcasted_iota(jnp.int32, (NB, NB), 1)
    return jnp.where(row_ids <= col_ids, chosen, chosen.T).astype(jnp.int32)


def draw_branch(key, part):
    key = jax.random.fold_in(key, 13)
    picks = jax.random.randint(key, (STEPS,), 0, 2).astype(jnp.int32)
    positions = lax.broadcasted_iota(jnp.int32, (STEPS,), 0)
    return jnp.where(positions == STEPS - 1, 1 - picks[0], picks).astype(jnp.int32)


def setup_inputs(seed: int = 0) -> dict:
    splits = jax.random.split(jax.random.key(seed), 4)
    return {
        "density": draw_density(jax.random.fold_in(splits[3], 71), 0),
        "pattern": draw_pattern(jax.random.fold_in(splits[3], 71), 0),
        "branch": draw_branch(jax.random.fold_in(splits[3], 71), 0),
    }


def reference(density, pattern, branch):
    tile_mask = jnp.maximum(pattern, jnp.eye(NB, dtype=jnp.int32))
    on_pattern = jnp.repeat(jnp.repeat(tile_mask, TILE, axis=0), TILE, axis=1).astype(jnp.float32)
    current = density * on_pattern
    for step in range(STEPS):
        squared = jnp.dot(current, current, precision=lax.Precision.HIGHEST, preferred_element_type=jnp.float32)
        current = on_pattern * jnp.where(branch[step] == 1, squared, 2.0 * current - squared)
    return current
```

```python
import jax
import jax.numpy as jnp
from jax import lax
from jax.sharding import PartitionSpec as P

TILE = 128
STEPS = 4


def exchange(parts, axis, groups=None):
    return lax.all_to_all(parts, axis, 0, 0, axis_index_groups=groups, tiled=True)


def gather(part, axis, members, groups=None):
    return exchange(jnp.broadcast_to(part[None], (members,) + part.shape), axis, groups)


def local(density, pattern, branch):
    rows, cols = lax.axis_size("row"), lax.axis_size("col")
    layers = lax.axis_size("depth")
    row, col, layer = lax.axis_index("row"), lax.axis_index("col"), lax.axis_index("depth")
    height, width = density.shape
    sub = width // layers
    core = row % 2
    cores_apart = [[x * 2 + c for x in range(rows // 2)] for c in range(2)]
    other_core = [(i, i ^ 1) for i in range(rows)]
    far = [[c + 4 * m for m in range(cols // 4)] for c in range(4)]

    row_ids = lax.broadcasted_iota(jnp.int32, pattern.shape, 0) + row * pattern.shape[0]
    col_ids = lax.broadcasted_iota(jnp.int32, pattern.shape, 1) + col * pattern.shape[1]
    tiles = jnp.where(row_ids == col_ids, 1, pattern).T.astype(jnp.float32)
    keep = jnp.repeat(jnp.repeat(tiles, TILE, axis=0), TILE, axis=1)
    keep_part = lax.dynamic_slice_in_dim(keep, layer * sub, sub, 0)

    def shifted(parts, by):
        return lax.ppermute(parts, "col", [(z, (z + by) % cols) for z in range(cols)])

    panel = density.T * keep
    part = lax.dynamic_slice_in_dim(panel, layer * sub, sub, 0)
    for step in range(STEPS):
        mine = panel.T.reshape(height // width, layers, sub, width)
        mine = lax.dynamic_index_in_dim(mine, layer, 1, keepdims=False)
        own = gather(mine, "row", rows // 2, cores_apart)
        other = lax.ppermute(own, "row", other_core)

        def product(left):
            out = jnp.dot(
                left.reshape(-1, width), panel, precision=lax.Precision.HIGH, preferred_element_type=jnp.float32
            )
            return out.reshape(rows // 2, 2, sub, height)

        both = jnp.stack([product(own), product(other)])

        def of_class(k):
            k = k % 4
            out = lax.dynamic_slice(
                both, ((k // 2) ^ core, 0, k % 2, 0, 0), (1, rows // 2, 1, sub, height)
            )
            return out.reshape(rows // 2, sub, height)

        up, down, across = of_class(col + 1), of_class(col + 3), of_class(col + 2)
        near = of_class(col)
        near = near + shifted(up, 1) + shifted(down, -1)
        near = near + jnp.concatenate([shifted(across[:2], 2), shifted(across[2:], -2)])
        squared = exchange(near, "col", far).reshape(cols // 4, sub, height).sum(0)
        part = keep_part * jnp.where(branch[step] == 1, squared, 2.0 * part - squared)
        panel = gather(part, "depth", layers).reshape(width, height)
    return panel.T


def solution(mesh):
    in_specs = (P("row", "col"), P("row", "col"), P())
    out_specs = P("row", "col")
    return jax.shard_map(local, mesh=mesh, in_specs=in_specs, out_specs=out_specs, check_vma=False)
```

```python
import functools

import jax
import jax.numpy as jnp
from jax import lax
from jax.experimental import pallas as pl
from jax.experimental.pallas import tpu as pltpu
from jax.sharding import PartitionSpec as P

TILE = 128
STEPS = 4
LANES = 8
NATURAL = 18
BALANCED = 14


def exchange(parts, axis, groups=None):
    return lax.all_to_all(parts, axis, 0, 0, axis_index_groups=groups, tiled=True)


def gather(part, axis, members, groups=None):
    return exchange(jnp.broadcast_to(part[None], (members,) + part.shape), axis, groups)


def shifted(parts, by):
    cols = lax.axis_size("col")
    return lax.ppermute(parts, "col", [(z, (z + by) % cols) for z in range(cols)])


def sum_along_col(ahead):
    cols = lax.axis_size("col")
    far = [[c + 4 * m for m in range(cols // 4)] for c in range(4)]
    near = ahead[0] + shifted(ahead[1], 1) + shifted(ahead[3], -1)
    near = near + jnp.concatenate([shifted(ahead[2][:2], 2), shifted(ahead[2][2:], -2)])
    return exchange(near, "col", far).sum(0)


def swap_cores(value):
    return lax.ppermute(value, "row", [(i, i ^ 1) for i in range(lax.axis_size("row"))])


def dense(density, pattern, branch):
    rows, cols = lax.axis_size("row"), lax.axis_size("col")
    layers = lax.axis_size("depth")
    row, col, layer = lax.axis_index("row"), lax.axis_index("col"), lax.axis_index("depth")
    height, width = density.shape
    sub = width // layers
    core = row % 2
    cores_apart = [[x * 2 + c for x in range(rows // 2)] for c in range(2)]

    row_ids = lax.broadcasted_iota(jnp.int32, pattern.shape, 0) + row * pattern.shape[0]
    col_ids = lax.broadcasted_iota(jnp.int32, pattern.shape, 1) + col * pattern.shape[1]
    tiles = jnp.where(row_ids == col_ids, 1, pattern).T.astype(jnp.float32)
    keep = jnp.repeat(jnp.repeat(tiles, TILE, axis=0), TILE, axis=1)
    keep_part = lax.dynamic_slice_in_dim(keep, layer * sub, sub, 0)

    panel = density.T * keep
    part = lax.dynamic_slice_in_dim(panel, layer * sub, sub, 0)
    for step in range(STEPS):
        mine = panel.T.reshape(height // width, layers, sub, width)
        mine = lax.dynamic_index_in_dim(mine, layer, 1, keepdims=False)
        own = gather(mine, "row", rows // 2, cores_apart)
        other = swap_cores(own)

        def product(left, panel=panel):
            out = jnp.dot(
                left.reshape(-1, width), panel, precision=lax.Precision.HIGH, preferred_element_type=jnp.float32
            )
            return out.reshape(rows // 2, 2, sub, height)

        both = jnp.stack([product(own), product(other)])

        def of_class(k, both=both):
            k = k % 4
            start = ((k // 2) ^ core, 0, k % 2, 0, 0)
            out = lax.dynamic_slice(both, start, (1, rows // 2, 1, sub, height))
            return out.reshape(rows // 2, sub, height)

        squared = sum_along_col([of_class(col + q) for q in range(4)])
        part = keep_part * jnp.where(branch[step] == 1, squared, 2.0 * part - squared)
        panel = gather(part, "depth", layers).reshape(width, height)
    return panel.T


def column_order(keep):
    n = keep.shape[0]
    load = keep.sum(0)
    ids = jnp.arange(n)
    ahead = (load[None, :] > load[:, None]) | ((load[None, :] == load[:, None]) & (ids[None, :] < ids[:, None]))
    rank = ahead.astype(jnp.int32).sum(1)
    place = jnp.where(rank < n // 2, 2 * rank, 2 * (n - 1 - rank) + 1)
    return jnp.where(place[None, :] == ids[:, None], ids[None, :], 0).sum(1)


def slot_lists(keep, order, slots):
    n = keep.shape[0]
    ids = jnp.arange(n)
    held = ((order[:, None] == ids[None, :])[:, :, None] & (keep[None, :, :] > 0)).any(1)
    held = held.reshape(n // 2, 2 * n)
    count = jnp.cumsum(held.astype(jnp.int32), axis=1)
    which = held[:, :, None] & (count[:, :, None] - 1 == jnp.arange(2 * slots)[None, None, :])
    spots = jnp.arange(2 * n)
    there = which.any(1)
    code = jnp.where(which, spots[None, :, None], 0).sum(1)
    source = order.reshape(n // 2, 2)[:, spots // n] * n + (spots % n)[None, :]
    source = jnp.where(which, source[:, :, None], 0).sum(1)
    return jnp.where(there, code, -1), jnp.where(there, source, -1), count[:, -1].max()


def pick_kernel(info_ref, from_ref, out_ref, *, slots, blocks):
    for t in range(slots):
        code = info_ref[t]
        at = jnp.maximum(code, 0)
        rows = pl.ds(pl.multiple_of((at // blocks) * LANES, LANES), LANES)
        lanes = pl.ds(pl.multiple_of((at % blocks) * TILE, TILE), TILE)
        out_ref[t * LANES : (t + 1) * LANES, :] = jnp.where(code >= 0, from_ref[rows, lanes], 0.0)


def place_kernel(info_ref, own_ref, other_ref, out_ref, *, slots, blocks):
    out_ref[...] = jnp.zeros_like(out_ref)
    for base, ref in ((0, own_ref), (slots, other_ref)):
        for t in range(slots):
            code = info_ref[base + t]

            @pl.when(code >= 0)
            def _(code=code, ref=ref, t=t):
                rows = pl.ds(pl.multiple_of((code // blocks) * LANES, LANES), LANES)
                lanes = pl.ds(pl.multiple_of((code % blocks) * TILE, TILE), TILE)
                out_ref[rows, lanes] = ref[t * LANES : (t + 1) * LANES, :]


def step_kernel(info_ref, own_ref, other_ref, out_ref, x_ref, hi_ref, lo_ref, left_hi, left_lo, prod_ref,
                *, slots_in, slots_out, blocks):
    share, square = info_ref[0], info_ref[3]
    sharers = TILE // LANES
    x_ref[...] = jnp.zeros_like(x_ref)
    for base, ref in ((4, own_ref), (4 + slots_in, other_ref)):

        def place(t, _, base=base, ref=ref):
            code = info_ref[base + t]

            @pl.when(code >= 0)
            def _():
                lanes = pl.ds(pl.multiple_of((code % blocks) * TILE, TILE), TILE)
                rows = pl.ds(pl.multiple_of(t * LANES, LANES), LANES)
                for s in range(sharers):
                    at = pl.multiple_of((code // blocks) * TILE + s * LANES, LANES)
                    x_ref[pl.ds(at, LANES), lanes] = ref[s, rows, :]

            return 0

        lax.fori_loop(0, slots_in, place, 0)

    one = lax.broadcasted_iota(jnp.int32, (LANES, TILE), 1) == share * LANES + lax.broadcasted_iota(
        jnp.int32, (LANES, TILE), 0
    )
    one = jnp.where(one, 1.0, 0.0).astype(jnp.bfloat16)
    across = (((1,), (1,)), ((), ()))
    for j in range(blocks):
        lanes = slice(j * TILE, (j + 1) * TILE)
        x = x_ref[:, lanes]
        hi = x.astype(jnp.bfloat16)
        lo = (x - hi.astype(jnp.float32)).astype(jnp.bfloat16)
        hi_ref[:, lanes] = hi
        lo_ref[:, lanes] = lo
        rows = slice(j * LANES, (j + 1) * LANES)
        left_hi[rows, :] = lax.dot_general(one, hi, across, preferred_element_type=jnp.float32)
        left_lo[rows, :] = lax.dot_general(one, lo, across, preferred_element_type=jnp.float32)
    a_hi = left_hi[...].astype(jnp.bfloat16)
    a_lo = left_lo[...].astype(jnp.bfloat16)
    wide = 4 * TILE
    for j in range(blocks * TILE // wide):
        lanes = slice(j * wide, (j + 1) * wide)
        b_hi, b_lo = hi_ref[:, lanes], lo_ref[:, lanes]
        prod_ref[:, lanes] = (
            jnp.dot(a_hi, b_hi, preferred_element_type=jnp.float32)
            + jnp.dot(a_hi, b_lo, preferred_element_type=jnp.float32)
            + jnp.dot(a_lo, b_hi, preferred_element_type=jnp.float32)
        )

    sign = jnp.where(square == 1, 1.0, -1.0)
    weight = jnp.where(square == 1, 0.0, -2.0)
    for half in range(2):
        rows = pl.ds(pl.multiple_of(info_ref[1 + half] * LANES, LANES), LANES)
        mine = pl.ds(pl.multiple_of(half * TILE + share * LANES, LANES), LANES)
        prod_ref[rows, :] = prod_ref[rows, :] + weight * x_ref[mine, :]

    first = 4 + 2 * slots_in

    def pick(t, _):
        code = info_ref[first + t]
        at = jnp.maximum(code, 0)
        rows = pl.ds(pl.multiple_of((at // blocks) * LANES, LANES), LANES)
        lanes = pl.ds(pl.multiple_of((at % blocks) * TILE, TILE), TILE)
        out = pl.ds(pl.multiple_of(t * LANES, LANES), LANES)
        out_ref[out, :] = jnp.where(code >= 0, sign * prod_ref[rows, lanes], 0.0)
        return 0

    lax.fori_loop(0, out_ref.shape[0] // LANES, pick, 0, unroll=8)


def on_core(kernel, shape, scratch=(), vmem=None):
    vmem_spec, smem_spec = pl.BlockSpec(memory_space=pltpu.VMEM), pl.BlockSpec(memory_space=pltpu.SMEM)

    def call(info, *arrays):
        return pl.pallas_call(
            kernel,
            out_shape=jax.ShapeDtypeStruct(shape, jnp.float32),
            in_specs=[smem_spec] + [vmem_spec] * len(arrays),
            out_specs=vmem_spec,
            scratch_shapes=list(scratch),
            compiler_params=pltpu.CompilerParams(vmem_limit_bytes=vmem),
        )(info, *arrays)

    return call


def sparse(strips, keep, lists, branch):
    rows, cols, layers = lax.axis_size("row"), lax.axis_size("col"), lax.axis_size("depth")
    row, col, layer = lax.axis_index("row"), lax.axis_index("col"), lax.axis_index("depth")
    core, share = row % 2, (row // 2) * layers + layer
    sharers, blocks = TILE // LANES, keep.shape[0]
    order = blocks * TILE
    in_plane = [
        [(x * 2 + c) * layers + y for x in range(rows // 2) for y in range(layers)] for c in range(2)
    ]
    bytes_limit = 48 * 1024 * 1024

    def of_plane(which, core):
        codes = lists[which][1].reshape(cols, 2, -1)
        return lax.dynamic_slice(codes, (col, core, 0), (1, 1, codes.shape[2])).reshape(-1)

    def for_planes(which):
        sources = lists[which][2].reshape(cols // 4, 4, 2, -1)
        sources = lax.dynamic_index_in_dim(sources, core, 2, keepdims=False)
        twice = jnp.concatenate([sources, sources], axis=1)
        return lax.dynamic_slice_in_dim(twice, col % 4, 4, 1).transpose(1, 0, 2).reshape(-1)

    natural = of_plane("natural", core)
    part = on_core(
        functools.partial(pick_kernel, slots=NATURAL, blocks=blocks), (NATURAL * LANES, TILE), vmem=bytes_limit
    )(natural, strips)
    layouts = ["natural"] + ["balanced"] * (STEPS - 1) + ["natural"]
    size = {"natural": NATURAL, "balanced": BALANCED}
    for step in range(STEPS):
        now, then = layouts[step], layouts[step + 1]
        own = gather(part, ("row", "depth"), sharers, in_plane)
        other = swap_cores(own)
        held = lax.dynamic_slice_in_dim(lists[now][0], 2 * col, 2, 0)
        info = jnp.concatenate(
            [share[None], held, branch[step][None], of_plane(now, core), of_plane(now, 1 - core), for_planes(then)]
        ).astype(jnp.int32)
        wide = 2 * TILE
        out = on_core(
            functools.partial(step_kernel, slots_in=size[now], slots_out=size[then], blocks=blocks),
            (cols * size[then] * LANES, TILE),
            scratch=(
                pltpu.VMEM((wide, order), jnp.float32),
                pltpu.VMEM((wide, order), jnp.bfloat16),
                pltpu.VMEM((wide, order), jnp.bfloat16),
                pltpu.VMEM((blocks * LANES, wide), jnp.float32),
                pltpu.VMEM((blocks * LANES, wide), jnp.float32),
                pltpu.VMEM((blocks * LANES, order), jnp.float32),
            ),
            vmem=bytes_limit,
        )(info, own, other)
        part = sum_along_col(out.reshape(4, cols // 4, size[then] * LANES, TILE))

    info = jnp.concatenate([natural, of_plane("natural", 1 - core)])
    strips = on_core(
        functools.partial(place_kernel, slots=NATURAL, blocks=blocks), strips.shape, vmem=bytes_limit
    )(info, part, swap_cores(part))
    height = order // rows
    cut = strips.reshape(2 * LANES, rows // 2, 2, height)
    cut = lax.dynamic_index_in_dim(cut, core, 2, keepdims=False).transpose(1, 0, 2)
    cut = jnp.broadcast_to(cut[:, None], (rows // 2, layers) + cut.shape[1:]).reshape(sharers, 2 * LANES, height)
    back = exchange(cut, ("row", "depth"), in_plane)
    back = back.reshape(sharers, 2, LANES, height).transpose(1, 0, 2, 3).reshape(2 * TILE, height)
    return back.T


def local(density, pattern, branch):
    rows, cols, layers = lax.axis_size("row"), lax.axis_size("col"), lax.axis_size("depth")
    layer = lax.axis_index("depth")
    height, width = density.shape
    blocks = rows * pattern.shape[0]
    cut = density.T.reshape(2, rows // 2, layers, LANES, height)
    cut = lax.dynamic_index_in_dim(cut, layer, 2, keepdims=False).transpose(1, 0, 2, 3)
    cut = cut.reshape(rows // 2, 2 * LANES, height)
    marks = jnp.zeros((LANES, height), jnp.float32).at[:2, : pattern.shape[0]].set(pattern.T.astype(jnp.float32))
    cut = jnp.concatenate([cut, jnp.broadcast_to(marks[None], (rows // 2,) + marks.shape)], axis=1)
    cut = jnp.broadcast_to(cut[:, None], (rows // 2, 2) + cut.shape[1:]).reshape((rows,) + cut.shape[1:])
    got = exchange(cut, "row")
    strips = got[:, : 2 * LANES].transpose(1, 0, 2).reshape(2 * LANES, rows * height)
    marks = got[:, 2 * LANES : 2 * LANES + 2, : pattern.shape[0]].transpose(1, 0, 2).reshape(2, blocks)
    marks = jnp.zeros((LANES, TILE), jnp.float32).at[:2, :blocks].set(marks)
    marks = gather(marks, "col", cols)[:, :2, :blocks].reshape(blocks, blocks)
    ids = jnp.arange(blocks)
    keep = jnp.where(ids[:, None] == ids[None, :], 1, marks.astype(jnp.int32))
    lists, fits = {}, True
    for name, order, slots in (("natural", ids, NATURAL), ("balanced", column_order(keep), BALANCED)):
        code, source, most = slot_lists(keep, order, slots)
        lists[name] = (order, code, source)
        fits = fits & (most <= 2 * slots)
    return lax.cond(
        fits,
        lambda: sparse(strips, keep, lists, branch),
        lambda: dense(density, pattern, branch),
    )


def solution(mesh):
    in_specs = (P("row", "col"), P("row", "col"), P())
    out_specs = P("row", "col")
    return jax.shard_map(local, mesh=mesh, in_specs=in_specs, out_specs=out_specs, check_vma=False)
```

```python
import functools

import jax
import jax.numpy as jnp
from jax import lax
from jax.experimental import pallas as pl
from jax.experimental.pallas import tpu as pltpu
from jax.sharding import PartitionSpec as P

TILE = 128
STEPS = 4
LANES = 8
NATURAL = 18
BALANCED = (12, 13, 14)


def exchange(parts, axis, groups=None):
    return lax.all_to_all(parts, axis, 0, 0, axis_index_groups=groups, tiled=True)


def gather(part, axis, members, groups=None):
    return exchange(jnp.broadcast_to(part[None], (members,) + part.shape), axis, groups)


def shifted(parts, by):
    cols = lax.axis_size("col")
    return lax.ppermute(parts, "col", [(z, (z + by) % cols) for z in range(cols)])


def sum_along_col(ahead):
    cols = lax.axis_size("col")
    far = [[c + 4 * m for m in range(cols // 4)] for c in range(4)]
    near = ahead[0] + shifted(ahead[1], 1) + shifted(ahead[3], -1)
    near = near + jnp.concatenate([shifted(ahead[2][:2], 2), shifted(ahead[2][2:], -2)])
    return exchange(near, "col", far).sum(0)


def swap_cores(value):
    return lax.ppermute(value, "row", [(i, i ^ 1) for i in range(lax.axis_size("row"))])


def dense(density, pattern, branch):
    rows, cols = lax.axis_size("row"), lax.axis_size("col")
    layers = lax.axis_size("depth")
    row, col, layer = lax.axis_index("row"), lax.axis_index("col"), lax.axis_index("depth")
    height, width = density.shape
    sub = width // layers
    core = row % 2
    cores_apart = [[x * 2 + c for x in range(rows // 2)] for c in range(2)]

    row_ids = lax.broadcasted_iota(jnp.int32, pattern.shape, 0) + row * pattern.shape[0]
    col_ids = lax.broadcasted_iota(jnp.int32, pattern.shape, 1) + col * pattern.shape[1]
    tiles = jnp.where(row_ids == col_ids, 1, pattern).T.astype(jnp.float32)
    keep = jnp.repeat(jnp.repeat(tiles, TILE, axis=0), TILE, axis=1)
    keep_part = lax.dynamic_slice_in_dim(keep, layer * sub, sub, 0)

    panel = density.T * keep
    part = lax.dynamic_slice_in_dim(panel, layer * sub, sub, 0)
    for step in range(STEPS):
        mine = panel.T.reshape(height // width, layers, sub, width)
        mine = lax.dynamic_index_in_dim(mine, layer, 1, keepdims=False)
        own = gather(mine, "row", rows // 2, cores_apart)
        other = swap_cores(own)

        def product(left, panel=panel):
            out = jnp.dot(
                left.reshape(-1, width), panel, precision=lax.Precision.HIGH, preferred_element_type=jnp.float32
            )
            return out.reshape(rows // 2, 2, sub, height)

        both = jnp.stack([product(own), product(other)])

        def of_class(k, both=both):
            k = k % 4
            start = ((k // 2) ^ core, 0, k % 2, 0, 0)
            out = lax.dynamic_slice(both, start, (1, rows // 2, 1, sub, height))
            return out.reshape(rows // 2, sub, height)

        squared = sum_along_col([of_class(col + q) for q in range(4)])
        part = keep_part * jnp.where(branch[step] == 1, squared, 2.0 * part - squared)
        panel = gather(part, "depth", layers).reshape(width, height)
    return panel.T


def column_order(keep):
    n = keep.shape[0]
    load = keep.sum(0)
    ids = jnp.arange(n)
    ahead = (load[None, :] > load[:, None]) | ((load[None, :] == load[:, None]) & (ids[None, :] < ids[:, None]))
    rank = ahead.astype(jnp.int32).sum(1)
    place = jnp.where(rank < n // 2, 2 * rank, 2 * (n - 1 - rank) + 1)
    return jnp.where(place[None, :] == ids[:, None], ids[None, :], 0).sum(1)


def slot_list(held, columns, slots):
    n = held.shape[-1]
    ids = jnp.arange(n)
    upto = (ids[:, None] <= ids[None, :]).astype(jnp.float32)
    count = jnp.dot(held.astype(jnp.float32), upto).astype(jnp.int32)
    which = jnp.arange(2)[:, None]
    place = count - 1 + which * count[..., :1, -1:]
    value = 1 + 2 * n * (n * columns[..., None] + ids) + n * which + ids
    hit = (held > 0)[..., None] & (place[..., None] == jnp.arange(2 * slots))
    return jnp.where(hit, value[..., None], 0).sum((-3, -2))


def spot(packed, blocks, in_product):
    at = jnp.maximum(packed - 1, 0)
    at = at >> blocks.bit_length() if in_product else at & (2 * blocks - 1)
    return at >> (blocks.bit_length() - 1), pl.ds(pl.multiple_of((at & (blocks - 1)) * TILE, TILE), TILE)


def pick_kernel(info_ref, from_ref, out_ref, *, slots, blocks):
    for t in range(slots):
        block, lanes = spot(info_ref[t], blocks, False)
        rows = pl.ds(pl.multiple_of(block * LANES, LANES), LANES)
        out_ref[t * LANES : (t + 1) * LANES, :] = jnp.where(info_ref[t] > 0, from_ref[rows, lanes], 0.0)


def place_kernel(info_ref, own_ref, other_ref, out_ref, *, slots, blocks):
    out_ref[...] = jnp.zeros_like(out_ref)
    for base, ref in ((0, own_ref), (slots, other_ref)):
        for t in range(slots):
            block, lanes = spot(info_ref[base + t], blocks, False)

            @pl.when(info_ref[base + t] > 0)
            def _(block=block, lanes=lanes, ref=ref, t=t):
                rows = pl.ds(pl.multiple_of(block * LANES, LANES), LANES)
                out_ref[rows, lanes] = ref[t * LANES : (t + 1) * LANES, :]


def step_kernel(info_ref, own_ref, other_ref, out_ref, x_ref, hi_ref, lo_ref, left_ref, prod_ref,
                *, slots_in, slots_out, blocks):
    share, square = info_ref[0], info_ref[3]
    sharers = TILE // LANES
    x_ref[...] = jnp.zeros_like(x_ref)
    for base, ref in ((4, own_ref), (4 + slots_in, other_ref)):

        def place(t, _, base=base, ref=ref):
            block, lanes = spot(info_ref[base + t], blocks, False)

            @pl.when(info_ref[base + t] > 0)
            def _():
                rows = pl.ds(pl.multiple_of(t * LANES, LANES), LANES)
                for s in range(sharers):
                    at = pl.multiple_of(block * TILE + s * LANES, LANES)
                    x_ref[pl.ds(at, LANES), lanes] = ref[s, rows, :]

            return 0

        lax.fori_loop(0, slots_in, place, 0)

    group = lax.broadcasted_iota(jnp.int32, (x_ref.shape[0], TILE), 1) // LANES
    for j in range(blocks):
        lanes = slice(j * TILE, (j + 1) * TILE)
        x = x_ref[:, lanes]
        hi = x.astype(jnp.bfloat16)
        hi_ref[:, lanes] = hi
        lo_ref[:, lanes] = (x - hi.astype(jnp.float32)).astype(jnp.bfloat16)
        half = slice(j // sharers * TILE, (j // sharers + 1) * TILE)
        turned = pltpu.roll(x, ((j - share) & (sharers - 1)) * LANES, 1)
        left_ref[:, half] = jnp.where(group == j % sharers, turned, left_ref[:, half])
    left = left_ref[...].T
    a_hi = left.astype(jnp.bfloat16)
    a_lo = (left - a_hi.astype(jnp.float32)).astype(jnp.bfloat16)
    wide = 4 * TILE
    for j in range(blocks * TILE // wide):
        lanes = slice(j * wide, (j + 1) * wide)
        b_hi, b_lo = hi_ref[:, lanes], lo_ref[:, lanes]
        prod_ref[:, lanes] = (
            jnp.dot(a_hi, b_hi, preferred_element_type=jnp.float32)
            + jnp.dot(a_hi, b_lo, preferred_element_type=jnp.float32)
            + jnp.dot(a_lo, b_hi, preferred_element_type=jnp.float32)
        )

    sign = jnp.where(square == 1, 1.0, -1.0)
    weight = jnp.where(square == 1, 0.0, -2.0)
    for half in range(2):
        rows = pl.ds(pl.multiple_of(info_ref[1 + half] * LANES, LANES), LANES)
        mine = pl.ds(pl.multiple_of(half * TILE + share * LANES, LANES), LANES)
        prod_ref[rows, :] = prod_ref[rows, :] + weight * x_ref[mine, :]

    first = 4 + 2 * slots_in

    def pick(t, _):
        packed = info_ref[first + t]
        block, lanes = spot(packed, blocks, True)
        rows = pl.ds(pl.multiple_of(block * LANES, LANES), LANES)
        out = pl.ds(pl.multiple_of(t * LANES, LANES), LANES)
        out_ref[out, :] = jnp.where(packed > 0, sign * prod_ref[rows, lanes], 0.0)
        return 0

    lax.fori_loop(0, out_ref.shape[0] // LANES, pick, 0, unroll=8)


def on_core(kernel, shape, scratch=()):
    vmem_spec, smem_spec = pl.BlockSpec(memory_space=pltpu.VMEM), pl.BlockSpec(memory_space=pltpu.SMEM)

    def call(info, *arrays):
        return pl.pallas_call(
            kernel,
            out_shape=jax.ShapeDtypeStruct(shape, jnp.float32),
            in_specs=[smem_spec] + [vmem_spec] * len(arrays),
            out_specs=vmem_spec,
            scratch_shapes=list(scratch),
            compiler_params=pltpu.CompilerParams(vmem_limit_bytes=48 * 1024 * 1024),
        )(info, *arrays)

    return call


def plane_groups():
    rows, layers = lax.axis_size("row"), lax.axis_size("depth")
    return [[(x * 2 + c) * layers + y for x in range(rows // 2) for y in range(layers)] for c in range(2)]


def in_plane(part):
    own = gather(part, ("row", "depth"), TILE // LANES, plane_groups())
    return own, swap_cores(own)


def sparse(slots, own, other, natural, balanced, order, branch):
    rows, cols, layers = lax.axis_size("row"), lax.axis_size("col"), lax.axis_size("depth")
    row, col, layer = lax.axis_index("row"), lax.axis_index("col"), lax.axis_index("depth")
    core, share = row % 2, (row // 2) * layers + layer
    blocks = order.shape[0]
    whole = blocks * TILE
    layouts = [(natural, NATURAL, jnp.arange(blocks))] + [(balanced, slots, order)] * (STEPS - 1)
    layouts = layouts + [layouts[0]]

    def of_plane(packed):
        packed = packed.reshape(cols, 2, -1)
        both = lax.dynamic_index_in_dim(packed, col, 0, keepdims=False)
        return jnp.where(core == 0, both, both[::-1]).reshape(-1)

    def for_planes(packed):
        packed = packed.reshape(cols // 4, 4, 2, -1)
        packed = lax.dynamic_index_in_dim(packed, core, 2, keepdims=False)
        twice = jnp.concatenate([packed, packed], axis=1)
        return lax.dynamic_slice_in_dim(twice, col % 4, 4, 1).transpose(1, 0, 2).reshape(-1)

    for step in range(STEPS):
        now, slots_in, columns = layouts[step]
        then, slots_out, _ = layouts[step + 1]
        if step > 0:
            own, other = in_plane(part)
        info = jnp.concatenate(
            [
                share[None],
                lax.dynamic_slice_in_dim(columns, 2 * col, 2, 0),
                branch[step][None],
                of_plane(now),
                for_planes(then),
            ]
        ).astype(jnp.int32)
        wide = 2 * TILE
        out = on_core(
            functools.partial(step_kernel, slots_in=slots_in, slots_out=slots_out, blocks=blocks),
            (cols * slots_out * LANES, TILE),
            scratch=(
                pltpu.VMEM((wide, whole), jnp.float32),
                pltpu.VMEM((wide, whole), jnp.bfloat16),
                pltpu.VMEM((wide, whole), jnp.bfloat16),
                pltpu.VMEM((wide, blocks * LANES), jnp.float32),
                pltpu.VMEM((blocks * LANES, whole), jnp.float32),
            ),
        )(info, own, other)
        part = sum_along_col(out.reshape(4, cols // 4, slots_out * LANES, TILE))

    strips = on_core(
        functools.partial(place_kernel, slots=NATURAL, blocks=blocks), (2 * LANES, whole)
    )(of_plane(natural), part, swap_cores(part))
    sharers, height = TILE // LANES, whole // rows
    cut = strips.reshape(2 * LANES, rows // 2, 2, height)
    cut = lax.dynamic_index_in_dim(cut, core, 2, keepdims=False).transpose(1, 0, 2)
    cut = jnp.broadcast_to(cut[:, None], (rows // 2, layers) + cut.shape[1:]).reshape(sharers, 2 * LANES, height)
    back = exchange(cut, ("row", "depth"), plane_groups())
    back = back.reshape(sharers, 2, LANES, height).transpose(1, 0, 2, 3).reshape(2 * TILE, height)
    return back.T


def local(density, pattern, branch):
    rows, cols, layers = lax.axis_size("row"), lax.axis_size("col"), lax.axis_size("depth")
    row, col, layer = lax.axis_index("row"), lax.axis_index("col"), lax.axis_index("depth")
    height, width = density.shape
    blocks = rows * pattern.shape[0]
    cut = density.T.reshape(2, rows // 2, layers, LANES, height)
    cut = lax.dynamic_index_in_dim(cut, layer, 2, keepdims=False).transpose(1, 0, 2, 3)
    cut = cut.reshape(rows // 2, 2 * LANES, height)
    marks = jnp.zeros((LANES, height), jnp.float32).at[:2, : pattern.shape[0]].set(pattern.T.astype(jnp.float32))
    cut = jnp.concatenate([cut, jnp.broadcast_to(marks[None], (rows // 2,) + marks.shape)], axis=1)
    cut = jnp.broadcast_to(cut[:, None], (rows // 2, 2) + cut.shape[1:]).reshape((rows,) + cut.shape[1:])
    got = exchange(cut, "row")
    strips = got[:, : 2 * LANES].transpose(1, 0, 2).reshape(2 * LANES, rows * height)
    marks = got[:, 2 * LANES : 2 * LANES + 2, : pattern.shape[0]].transpose(1, 0, 2).reshape(2, blocks)

    ids = jnp.arange(blocks)
    sent = jnp.zeros((LANES, TILE), jnp.float32).at[:2, :blocks].set(marks)
    sent = lax.all_gather(sent, "col", axis=0, tiled=True)
    columns = 2 * col + jnp.arange(2)
    held = jnp.where(columns[:, None] == ids, 1, marks.astype(jnp.int32))
    mine = slot_list(held, columns, NATURAL).reshape(2, NATURAL)
    part = on_core(functools.partial(pick_kernel, slots=NATURAL, blocks=blocks), (NATURAL * LANES, TILE))(
        lax.dynamic_index_in_dim(mine, row % 2, 0, keepdims=False), strips
    )
    own, other = in_plane(part)

    sent = sent.reshape(cols, LANES, TILE)[:, :2, :blocks].reshape(blocks, blocks)
    keep = jnp.where(ids[:, None] == ids[None, :], 1, sent.astype(jnp.int32))
    order = column_order(keep)
    moved = jnp.dot((order[:, None] == ids).astype(jnp.float32), keep.astype(jnp.float32)).astype(jnp.int32)

    def in_pairs(rows_of):
        return rows_of.reshape((cols, 2) + rows_of.shape[1:])

    natural = slot_list(in_pairs(keep), in_pairs(ids), NATURAL)
    most = in_pairs(moved).sum((1, 2)).max()
    too_many = in_pairs(keep).sum((1, 2)).max() > 2 * NATURAL
    size = sum((most > 2 * slots).astype(jnp.int32) for slots in BALANCED)

    def of_size(slots):
        def run():
            balanced = slot_list(in_pairs(moved), in_pairs(order), slots)
            return sparse(slots, own, other, natural, balanced, order, branch)

        return run

    return lax.switch(
        jnp.where(too_many, len(BALANCED), size),
        [of_size(slots) for slots in BALANCED] + [lambda: dense(density, pattern, branch)],
    )


def solution(mesh):
    in_specs = (P("row", "col"), P("row", "col"), P())
    out_specs = P("row", "col")
    return jax.shard_map(local, mesh=mesh, in_specs=in_specs, out_specs=out_specs, check_vma=False)
```

```python
import functools

import jax
import jax.numpy as jnp
from jax import lax
from jax.experimental import pallas as pl
from jax.experimental.pallas import tpu as pltpu
from jax.sharding import PartitionSpec as P

TILE = 128
STEPS = 4
LANES = 8
NATURAL = 18
BALANCED = 14


def exchange(parts, axis, groups=None):
    return lax.all_to_all(parts, axis, 0, 0, axis_index_groups=groups, tiled=True)


def gather(part, axis, members, groups=None):
    return exchange(jnp.broadcast_to(part[None], (members,) + part.shape), axis, groups)


def shifted(parts, by):
    cols = lax.axis_size("col")
    return lax.ppermute(parts, "col", [(z, (z + by) % cols) for z in range(cols)])


def sum_along_col(ahead):
    cols = lax.axis_size("col")
    half = cols // 4
    apart = [[c + 2 * m for m in range(cols // 2)] for c in range(2)]
    near = ahead[0] + jnp.concatenate([shifted(ahead[1][:half], 1), shifted(ahead[1][half:], -1)])
    return exchange(near, "col", apart).sum(0)


def swap_cores(value):
    return lax.ppermute(value, "row", [(i, i ^ 1) for i in range(lax.axis_size("row"))])


def dense(density, pattern, branch):
    rows, cols = lax.axis_size("row"), lax.axis_size("col")
    layers = lax.axis_size("depth")
    row, col, layer = lax.axis_index("row"), lax.axis_index("col"), lax.axis_index("depth")
    height, width = density.shape
    sub = width // layers
    core = row % 2
    cores_apart = [[x * 2 + c for x in range(rows // 2)] for c in range(2)]

    row_ids = lax.broadcasted_iota(jnp.int32, pattern.shape, 0) + row * pattern.shape[0]
    col_ids = lax.broadcasted_iota(jnp.int32, pattern.shape, 1) + col * pattern.shape[1]
    tiles = jnp.where(row_ids == col_ids, 1, pattern).T.astype(jnp.float32)
    keep = jnp.repeat(jnp.repeat(tiles, TILE, axis=0), TILE, axis=1)
    keep_part = lax.dynamic_slice_in_dim(keep, layer * sub, sub, 0)

    panel = density.T * keep
    part = lax.dynamic_slice_in_dim(panel, layer * sub, sub, 0)
    for step in range(STEPS):
        mine = panel.T.reshape(height // width, layers, sub, width)
        mine = lax.dynamic_index_in_dim(mine, layer, 1, keepdims=False)
        own = gather(mine, "row", rows // 2, cores_apart)
        other = swap_cores(own)

        def product(left, panel=panel):
            out = jnp.dot(
                left.reshape(-1, width), panel, precision=lax.Precision.HIGH, preferred_element_type=jnp.float32
            )
            return out.reshape(rows // 2, 2, sub, height)

        mine, others = product(own), product(other)
        both = lax.dynamic_slice_in_dim(jnp.stack([mine, others, mine]), core, 2, 0).transpose(1, 0, 2, 3, 4)
        both = both.reshape(rows, 2, sub, height)
        both = jnp.concatenate([both, both], axis=1)
        squared = sum_along_col(lax.dynamic_slice_in_dim(both, col % 2, 2, 1).transpose(1, 0, 2, 3))
        part = keep_part * jnp.where(branch[step] == 1, squared, 2.0 * part - squared)
        panel = gather(part, "depth", layers).reshape(width, height)
    return panel.T


def column_order(keep):
    n = keep.shape[0]
    load = keep.sum(0)
    ids = jnp.arange(n)
    ahead = (load[None, :] > load[:, None]) | ((load[None, :] == load[:, None]) & (ids[None, :] < ids[:, None]))
    rank = ahead.astype(jnp.int32).sum(1)
    place = jnp.where(rank < n // 2, 2 * rank, 2 * (n - 1 - rank) + 1)
    return jnp.where(place[None, :] == ids[:, None], ids[None, :], 0).sum(1)


def slot_list(held, columns, slots):
    n = held.shape[-1]
    ids = jnp.arange(n)
    upto = (ids[:, None] <= ids[None, :]).astype(jnp.float32)
    count = jnp.dot(held.astype(jnp.float32), upto).astype(jnp.int32)
    which = jnp.arange(2)[:, None]
    place = count - 1 + which * count[..., :1, -1:]
    value = 1 + 2 * n * (n * columns[..., None] + ids) + n * which + ids
    hit = (held > 0)[..., None] & (place[..., None] == jnp.arange(2 * slots))
    return jnp.where(hit, value[..., None], 0).sum((-3, -2))


def spot(packed, blocks, in_product):
    at = jnp.maximum(packed - 1, 0)
    at = at >> blocks.bit_length() if in_product else at & (2 * blocks - 1)
    return at >> (blocks.bit_length() - 1), pl.ds(pl.multiple_of((at & (blocks - 1)) * TILE, TILE), TILE)


def pick_kernel(info_ref, from_ref, out_ref, *, slots, blocks):
    for t in range(slots):
        block, lanes = spot(info_ref[t], blocks, False)
        rows = pl.ds(pl.multiple_of(block * LANES, LANES), LANES)
        out_ref[t * LANES : (t + 1) * LANES, :] = jnp.where(info_ref[t] > 0, from_ref[rows, lanes], 0.0)


def place_kernel(info_ref, own_ref, other_ref, out_ref, *, slots, blocks):
    out_ref[...] = jnp.zeros_like(out_ref)
    for base, ref in ((0, own_ref), (slots, other_ref)):
        for t in range(slots):
            block, lanes = spot(info_ref[base + t], blocks, False)

            @pl.when(info_ref[base + t] > 0)
            def _(block=block, lanes=lanes, ref=ref, t=t):
                rows = pl.ds(pl.multiple_of(block * LANES, LANES), LANES)
                out_ref[rows, lanes] = ref[t * LANES : (t + 1) * LANES, :]


def step_kernel(info_ref, own_ref, other_ref, out_ref, x_ref, hi_ref, lo_ref, left_ref, left_hi, left_lo, prod_ref,
                *, slots_in, slots_out, blocks):
    share, square = info_ref[0], info_ref[3]
    sharers = TILE // LANES

    def clear(j, _):
        x_ref[:, pl.ds(pl.multiple_of(j * TILE, TILE), TILE)] = jnp.zeros((x_ref.shape[0], TILE), jnp.float32)
        return 0

    lax.fori_loop(0, blocks, clear, 0)
    for base, ref in ((4, own_ref), (4 + slots_in, other_ref)):

        def place(t, _, base=base, ref=ref):
            block, lanes = spot(info_ref[base + t], blocks, False)

            @pl.when(info_ref[base + t] > 0)
            def _():
                rows = pl.ds(pl.multiple_of(t * LANES, LANES), LANES)
                for s in range(sharers):
                    at = pl.multiple_of(block * TILE + s * LANES, LANES)
                    x_ref[pl.ds(at, LANES), lanes] = ref[s, rows, :]

            return 0

        lax.fori_loop(0, slots_in, place, 0)

    group = lax.broadcasted_iota(jnp.int32, (x_ref.shape[0], TILE), 1) // LANES

    def split(j, _):
        lanes = pl.ds(pl.multiple_of(j * TILE, TILE), TILE)
        x = x_ref[:, lanes]
        hi = x.astype(jnp.bfloat16)
        hi_ref[:, lanes] = hi
        lo_ref[:, lanes] = (x - hi.astype(jnp.float32)).astype(jnp.bfloat16)
        half = pl.ds(pl.multiple_of(j // sharers * TILE, TILE), TILE)
        turned = pltpu.roll(x, ((j - share) & (sharers - 1)) * LANES, 1)
        left_ref[:, half] = jnp.where(group == (j & (sharers - 1)), turned, left_ref[:, half])
        return 0

    lax.fori_loop(0, blocks, split, 0)
    left = left_ref[...].T
    a_hi = left.astype(jnp.bfloat16)
    left_hi[...] = a_hi
    left_lo[...] = (left - a_hi.astype(jnp.float32)).astype(jnp.bfloat16)
    wide = 4 * TILE

    def multiply(j, _):
        lanes = pl.ds(pl.multiple_of(j * wide, wide), wide)
        a_hi, a_lo, b_hi, b_lo = left_hi[...], left_lo[...], hi_ref[:, lanes], lo_ref[:, lanes]
        prod_ref[:, lanes] = (
            jnp.dot(a_hi, b_hi, preferred_element_type=jnp.float32)
            + jnp.dot(a_hi, b_lo, preferred_element_type=jnp.float32)
            + jnp.dot(a_lo, b_hi, preferred_element_type=jnp.float32)
        )
        return 0

    lax.fori_loop(0, blocks * TILE // wide, multiply, 0)

    sign = jnp.where(square == 1, 1.0, -1.0)
    weight = jnp.where(square == 1, 0.0, -2.0)
    for half in range(2):
        rows = pl.ds(pl.multiple_of(info_ref[1 + half] * LANES, LANES), LANES)
        mine = pl.ds(pl.multiple_of(half * TILE + share * LANES, LANES), LANES)
        prod_ref[rows, :] = prod_ref[rows, :] + weight * x_ref[mine, :]

    first = 4 + 2 * slots_in

    def pick(t, _):
        packed = info_ref[first + t]
        block, lanes = spot(packed, blocks, True)
        rows = pl.ds(pl.multiple_of(block * LANES, LANES), LANES)
        out = pl.ds(pl.multiple_of(t * LANES, LANES), LANES)
        out_ref[out, :] = jnp.where(packed > 0, sign * prod_ref[rows, lanes], 0.0)
        return 0

    lax.fori_loop(0, out_ref.shape[0] // LANES, pick, 0, unroll=4)


def on_core(kernel, shape, scratch=()):
    vmem_spec, smem_spec = pl.BlockSpec(memory_space=pltpu.VMEM), pl.BlockSpec(memory_space=pltpu.SMEM)

    def call(info, *arrays):
        return pl.pallas_call(
            kernel,
            out_shape=jax.ShapeDtypeStruct(shape, jnp.float32),
            in_specs=[smem_spec] + [vmem_spec] * len(arrays),
            out_specs=vmem_spec,
            scratch_shapes=list(scratch),
            compiler_params=pltpu.CompilerParams(vmem_limit_bytes=48 * 1024 * 1024),
        )(info, *arrays)

    return call


def plane_groups():
    rows, layers = lax.axis_size("row"), lax.axis_size("depth")
    return [[(x * 2 + c) * layers + y for x in range(rows // 2) for y in range(layers)] for c in range(2)]


def in_plane(part):
    own = gather(part, ("row", "depth"), TILE // LANES, plane_groups())
    return own, swap_cores(own)


def sparse(own, other, natural, balanced, order, branch):
    rows, cols, layers = lax.axis_size("row"), lax.axis_size("col"), lax.axis_size("depth")
    row, col, layer = lax.axis_index("row"), lax.axis_index("col"), lax.axis_index("depth")
    core, share = row % 2, (row // 2) * layers + layer
    blocks = order.shape[0]
    whole = blocks * TILE
    layouts = [(natural, NATURAL, jnp.arange(blocks))] + [(balanced, BALANCED, order)] * (STEPS - 1)
    layouts = layouts + [layouts[0]]

    def of_plane(packed):
        packed = packed.reshape(cols, 2, -1)
        both = lax.dynamic_index_in_dim(packed, col, 0, keepdims=False)
        return jnp.where(core == 0, both, both[::-1]).reshape(-1)

    def for_planes(packed):
        packed = packed.reshape(cols // 2, 2, 2, -1)
        packed = lax.dynamic_index_in_dim(packed, core, 2, keepdims=False)
        twice = jnp.concatenate([packed, packed], axis=1)
        return lax.dynamic_slice_in_dim(twice, col % 2, 2, 1).transpose(1, 0, 2).reshape(-1)

    part = None
    for step in range(STEPS):
        now, slots_in, columns = layouts[step]
        then, slots_out, _ = layouts[step + 1]
        if step > 0:
            own, other = in_plane(part)
        info = jnp.concatenate(
            [
                share[None],
                lax.dynamic_slice_in_dim(columns, 2 * col, 2, 0),
                branch[step][None],
                of_plane(now),
                for_planes(then),
            ]
        ).astype(jnp.int32)
        wide = 2 * TILE
        out = on_core(
            functools.partial(step_kernel, slots_in=slots_in, slots_out=slots_out, blocks=blocks),
            (cols * slots_out * LANES, TILE),
            scratch=(
                pltpu.VMEM((wide, whole), jnp.float32),
                pltpu.VMEM((wide, whole), jnp.bfloat16),
                pltpu.VMEM((wide, whole), jnp.bfloat16),
                pltpu.VMEM((wide, blocks * LANES), jnp.float32),
                pltpu.VMEM((blocks * LANES, wide), jnp.bfloat16),
                pltpu.VMEM((blocks * LANES, wide), jnp.bfloat16),
                pltpu.VMEM((blocks * LANES, whole), jnp.float32),
            ),
        )(info, own, other)
        part = sum_along_col(out.reshape(2, cols // 2, slots_out * LANES, TILE))

    strips = on_core(
        functools.partial(place_kernel, slots=NATURAL, blocks=blocks), (2 * LANES, whole)
    )(of_plane(natural), part, swap_cores(part))
    sharers, height = TILE // LANES, whole // rows
    cut = strips.reshape(2 * LANES, rows // 2, 2, height)
    cut = lax.dynamic_index_in_dim(cut, core, 2, keepdims=False).transpose(1, 0, 2)
    cut = jnp.broadcast_to(cut[:, None], (rows // 2, layers) + cut.shape[1:]).reshape(sharers, 2 * LANES, height)
    back = exchange(cut, ("row", "depth"), plane_groups())
    back = back.reshape(sharers, 2, LANES, height).transpose(1, 0, 2, 3).reshape(2 * TILE, height)
    return back.T


def local(density, pattern, branch):
    rows, cols, layers = lax.axis_size("row"), lax.axis_size("col"), lax.axis_size("depth")
    row, col, layer = lax.axis_index("row"), lax.axis_index("col"), lax.axis_index("depth")
    height, width = density.shape
    blocks = rows * pattern.shape[0]
    cut = density.T.reshape(2, rows // 2, layers, LANES, height)
    cut = lax.dynamic_index_in_dim(cut, layer, 2, keepdims=False).transpose(1, 0, 2, 3)
    cut = cut.reshape(rows // 2, 2 * LANES, height)
    marks = jnp.zeros((LANES, height), jnp.float32).at[:2, : pattern.shape[0]].set(pattern.T.astype(jnp.float32))
    cut = jnp.concatenate([cut, jnp.broadcast_to(marks[None], (rows // 2,) + marks.shape)], axis=1)
    cut = jnp.broadcast_to(cut[:, None], (rows // 2, 2) + cut.shape[1:]).reshape((rows,) + cut.shape[1:])
    got = exchange(cut, "row")
    strips = got[:, : 2 * LANES].transpose(1, 0, 2).reshape(2 * LANES, rows * height)
    marks = got[:, 2 * LANES : 2 * LANES + 2, : pattern.shape[0]].transpose(1, 0, 2).reshape(2, blocks)

    ids = jnp.arange(blocks)
    sent = jnp.zeros((2, TILE), jnp.float32).at[:, :blocks].set(marks)
    ahead = jnp.concatenate(
        [
            lax.ppermute(
                sent,
                ("col", "depth"),
                [(z * layers + y, (z - layers * p - y) % cols * layers + y) for z in range(cols) for y in range(layers)],
            )
            for p in range(cols // layers)
        ]
    )
    columns = 2 * col + jnp.arange(2)
    held = jnp.where(columns[:, None] == ids, 1, marks.astype(jnp.int32))
    mine = slot_list(held, columns, NATURAL).reshape(2, NATURAL)
    part = on_core(functools.partial(pick_kernel, slots=NATURAL, blocks=blocks), (NATURAL * LANES, TILE))(
        lax.dynamic_index_in_dim(mine, row % 2, 0, keepdims=False), strips
    )
    own, other = in_plane(jnp.concatenate([part, ahead]))
    seen = own[:layers, NATURAL * LANES :, :blocks].reshape(layers, cols // layers, 2, blocks)
    seen = seen.transpose(1, 0, 2, 3).reshape(2 * cols, blocks)
    seen = jnp.concatenate([seen, seen])
    seen = lax.dynamic_slice_in_dim(seen, 2 * (cols - col), 2 * cols, 0)
    keep = jnp.where(ids[:, None] == ids[None, :], 1, seen.astype(jnp.int32))
    order = column_order(keep)
    moved = jnp.dot((order[:, None] == ids).astype(jnp.float32), keep.astype(jnp.float32)).astype(jnp.int32)

    def in_pairs(rows_of):
        return rows_of.reshape((cols, 2) + rows_of.shape[1:])

    natural = slot_list(in_pairs(keep), in_pairs(ids), NATURAL)
    balanced = slot_list(in_pairs(moved), in_pairs(order), BALANCED)
    spare = jnp.stack(
        [2 * NATURAL - in_pairs(keep).sum((1, 2)), 2 * BALANCED - in_pairs(moved).sum((1, 2))]
    )
    return lax.cond(
        spare.min() >= 0,
        lambda: sparse(own, other, natural, balanced, order, branch),
        lambda: dense(density, pattern, branch),
    )


def solution(mesh):
    in_specs = (P("row", "col"), P("row", "col"), P())
    out_specs = P("row", "col")
    return jax.shard_map(local, mesh=mesh, in_specs=in_specs, out_specs=out_specs, check_vma=False)
```

```python
import functools

import jax
import jax.numpy as jnp
from jax import lax
from jax.experimental import pallas as pl
from jax.experimental.pallas import tpu as pltpu
from jax.sharding import PartitionSpec as P

TILE = 128
STEPS = 4
LANES = 8
NATURAL = 18
BALANCED = 14


def exchange(parts, axis, groups=None):
    return lax.all_to_all(parts, axis, 0, 0, axis_index_groups=groups, tiled=True)


def gather(part, axis, members, groups=None):
    return exchange(jnp.broadcast_to(part[None], (members,) + part.shape), axis, groups)


def shifted(parts, by):
    cols = lax.axis_size("col")
    return lax.ppermute(parts, "col", [(z, (z + by) % cols) for z in range(cols)])


def sum_along_col(ahead):
    cols = lax.axis_size("col")
    far = [[c + 4 * m for m in range(cols // 4)] for c in range(4)]
    near = ahead[0] + shifted(ahead[1], 1) + shifted(ahead[3], -1)
    near = near + jnp.concatenate([shifted(ahead[2][:2], 2), shifted(ahead[2][2:], -2)])
    return exchange(near, "col", far).sum(0)


def swap_cores(value):
    return lax.ppermute(value, "row", [(i, i ^ 1) for i in range(lax.axis_size("row"))])


def dense(density, pattern, branch):
    rows, cols = lax.axis_size("row"), lax.axis_size("col")
    layers = lax.axis_size("depth")
    row, col, layer = lax.axis_index("row"), lax.axis_index("col"), lax.axis_index("depth")
    height, width = density.shape
    sub = width // layers
    core = row % 2
    cores_apart = [[x * 2 + c for x in range(rows // 2)] for c in range(2)]

    row_ids = lax.broadcasted_iota(jnp.int32, pattern.shape, 0) + row * pattern.shape[0]
    col_ids = lax.broadcasted_iota(jnp.int32, pattern.shape, 1) + col * pattern.shape[1]
    tiles = jnp.where(row_ids == col_ids, 1, pattern).T.astype(jnp.float32)
    keep = jnp.repeat(jnp.repeat(tiles, TILE, axis=0), TILE, axis=1)
    keep_part = lax.dynamic_slice_in_dim(keep, layer * sub, sub, 0)

    panel = density.T * keep
    part = lax.dynamic_slice_in_dim(panel, layer * sub, sub, 0)
    for step in range(STEPS):
        mine = panel.T.reshape(height // width, layers, sub, width)
        mine = lax.dynamic_index_in_dim(mine, layer, 1, keepdims=False)
        own = gather(mine, "row", rows // 2, cores_apart)
        other = swap_cores(own)

        def product(left, panel=panel):
            out = jnp.dot(
                left.reshape(-1, width), panel, precision=lax.Precision.HIGH, preferred_element_type=jnp.float32
            )
            return out.reshape(rows // 2, 2, sub, height)

        both = jnp.stack([product(own), product(other)])

        def of_class(k, both=both):
            k = k % 4
            start = ((k // 2) ^ core, 0, k % 2, 0, 0)
            out = lax.dynamic_slice(both, start, (1, rows // 2, 1, sub, height))
            return out.reshape(rows // 2, sub, height)

        squared = sum_along_col([of_class(col + q) for q in range(4)])
        part = keep_part * jnp.where(branch[step] == 1, squared, 2.0 * part - squared)
        panel = gather(part, "depth", layers).reshape(width, height)
    return panel.T


def column_order(keep):
    n = keep.shape[0]
    load = keep.sum(0)
    ids = jnp.arange(n)
    ahead = (load[None, :] > load[:, None]) | ((load[None, :] == load[:, None]) & (ids[None, :] < ids[:, None]))
    rank = ahead.astype(jnp.int32).sum(1)
    place = jnp.where(rank < n // 2, 2 * rank, 2 * (n - 1 - rank) + 1)
    return jnp.where(place[None, :] == ids[:, None], ids[None, :], 0).sum(1)


def slot_list(held, columns, slots):
    n = held.shape[-1]
    ids = jnp.arange(n)
    upto = (ids[:, None] <= ids[None, :]).astype(jnp.float32)
    count = jnp.dot(held.astype(jnp.float32), upto).astype(jnp.int32)
    which = jnp.arange(2)[:, None]
    place = count - 1 + which * count[..., :1, -1:]
    value = 1 + 2 * n * (n * columns[..., None] + ids) + n * which + ids
    hit = (held > 0)[..., None] & (place[..., None] == jnp.arange(2 * slots))
    return jnp.where(hit, value[..., None], 0).sum((-3, -2))


def spot(packed, blocks, in_product):
    at = jnp.maximum(packed - 1, 0)
    at = at >> blocks.bit_length() if in_product else at & (2 * blocks - 1)
    return at >> (blocks.bit_length() - 1), pl.ds(pl.multiple_of((at & (blocks - 1)) * TILE, TILE), TILE)


def pick_kernel(info_ref, from_ref, out_ref, *, slots, blocks):
    for t in range(slots):
        block, lanes = spot(info_ref[t], blocks, False)
        rows = pl.ds(pl.multiple_of(block * LANES, LANES), LANES)
        out_ref[t * LANES : (t + 1) * LANES, :] = jnp.where(info_ref[t] > 0, from_ref[rows, lanes], 0.0)


def place_kernel(info_ref, own_ref, other_ref, out_ref, *, slots, blocks):
    out_ref[...] = jnp.zeros_like(out_ref)
    for base, ref in ((0, own_ref), (slots, other_ref)):
        for t in range(slots):
            block, lanes = spot(info_ref[base + t], blocks, False)

            @pl.when(info_ref[base + t] > 0)
            def _(block=block, lanes=lanes, ref=ref, t=t):
                rows = pl.ds(pl.multiple_of(block * LANES, LANES), LANES)
                out_ref[rows, lanes] = ref[t * LANES : (t + 1) * LANES, :]


def step_kernel(info_ref, own_ref, other_ref, out_ref, x_ref, hi_ref, lo_ref, left_ref, prod_ref,
                *, slots_in, slots_out, blocks):
    share, square = info_ref[0], info_ref[3]
    sharers = TILE // LANES
    x_ref[...] = jnp.zeros_like(x_ref)
    for base, ref in ((4, own_ref), (4 + slots_in, other_ref)):

        def place(t, _, base=base, ref=ref):
            block, lanes = spot(info_ref[base + t], blocks, False)

            @pl.when(info_ref[base + t] > 0)
            def _():
                rows = pl.ds(pl.multiple_of(t * LANES, LANES), LANES)
                for s in range(sharers):
                    at = pl.multiple_of(block * TILE + s * LANES, LANES)
                    x_ref[pl.ds(at, LANES), lanes] = ref[s, rows, :]

            return 0

        lax.fori_loop(0, slots_in, place, 0)

    group = lax.broadcasted_iota(jnp.int32, (x_ref.shape[0], TILE), 1) // LANES
    for j in range(blocks):
        lanes = slice(j * TILE, (j + 1) * TILE)
        x = x_ref[:, lanes]
        hi = x.astype(jnp.bfloat16)
        hi_ref[:, lanes] = hi
        lo_ref[:, lanes] = (x - hi.astype(jnp.float32)).astype(jnp.bfloat16)
        half = slice(j // sharers * TILE, (j // sharers + 1) * TILE)
        turned = pltpu.roll(x, ((j - share) & (sharers - 1)) * LANES, 1)
        left_ref[:, half] = jnp.where(group == j % sharers, turned, left_ref[:, half])
    left = left_ref[...].T
    a_hi = left.astype(jnp.bfloat16)
    a_lo = (left - a_hi.astype(jnp.float32)).astype(jnp.bfloat16)
    wide = 4 * TILE
    for j in range(blocks * TILE // wide):
        lanes = slice(j * wide, (j + 1) * wide)
        b_hi, b_lo = hi_ref[:, lanes], lo_ref[:, lanes]
        prod_ref[:, lanes] = (
            jnp.dot(a_hi, b_hi, preferred_element_type=jnp.float32)
            + jnp.dot(a_hi, b_lo, preferred_element_type=jnp.float32)
            + jnp.dot(a_lo, b_hi, preferred_element_type=jnp.float32)
        )

    sign = jnp.where(square == 1, 1.0, -1.0)
    weight = jnp.where(square == 1, 0.0, -2.0)
    for half in range(2):
        rows = pl.ds(pl.multiple_of(info_ref[1 + half] * LANES, LANES), LANES)
        mine = pl.ds(pl.multiple_of(half * TILE + share * LANES, LANES), LANES)
        prod_ref[rows, :] = prod_ref[rows, :] + weight * x_ref[mine, :]

    first = 4 + 2 * slots_in

    def pick(t, _):
        packed = info_ref[first + t]
        block, lanes = spot(packed, blocks, True)
        rows = pl.ds(pl.multiple_of(block * LANES, LANES), LANES)
        out = pl.ds(pl.multiple_of(t * LANES, LANES), LANES)
        out_ref[out, :] = jnp.where(packed > 0, sign * prod_ref[rows, lanes], 0.0)
        return 0

    lax.fori_loop(0, out_ref.shape[0] // LANES, pick, 0, unroll=8)


def on_core(kernel, shape, scratch=()):
    vmem_spec, smem_spec = pl.BlockSpec(memory_space=pltpu.VMEM), pl.BlockSpec(memory_space=pltpu.SMEM)

    def call(info, *arrays):
        return pl.pallas_call(
            kernel,
            out_shape=jax.ShapeDtypeStruct(shape, jnp.float32),
            in_specs=[smem_spec] + [vmem_spec] * len(arrays),
            out_specs=vmem_spec,
            scratch_shapes=list(scratch),
            compiler_params=pltpu.CompilerParams(vmem_limit_bytes=48 * 1024 * 1024),
        )(info, *arrays)

    return call


def plane_groups():
    rows, layers = lax.axis_size("row"), lax.axis_size("depth")
    return [[(x * 2 + c) * layers + y for x in range(rows // 2) for y in range(layers)] for c in range(2)]


def in_plane(part):
    own = gather(part, ("row", "depth"), TILE // LANES, plane_groups())
    return own, swap_cores(own)


def sparse(own, other, natural, balanced, order, branch):
    rows, cols, layers = lax.axis_size("row"), lax.axis_size("col"), lax.axis_size("depth")
    row, col, layer = lax.axis_index("row"), lax.axis_index("col"), lax.axis_index("depth")
    core, share = row % 2, (row // 2) * layers + layer
    blocks = order.shape[0]
    whole = blocks * TILE
    layouts = [(natural, NATURAL, jnp.arange(blocks))] + [(balanced, BALANCED, order)] * (STEPS - 1)
    layouts = layouts + [layouts[0]]

    def of_plane(packed):
        packed = packed.reshape(cols, 2, -1)
        both = lax.dynamic_index_in_dim(packed, col, 0, keepdims=False)
        return jnp.where(core == 0, both, both[::-1]).reshape(-1)

    def for_planes(packed):
        packed = packed.reshape(cols // 4, 4, 2, -1)
        packed = lax.dynamic_index_in_dim(packed, core, 2, keepdims=False)
        twice = jnp.concatenate([packed, packed], axis=1)
        return lax.dynamic_slice_in_dim(twice, col % 4, 4, 1).transpose(1, 0, 2).reshape(-1)

    part = None
    for step in range(STEPS):
        now, slots_in, columns = layouts[step]
        then, slots_out, _ = layouts[step + 1]
        if step > 0:
            own, other = in_plane(part)
        info = jnp.concatenate(
            [
                share[None],
                lax.dynamic_slice_in_dim(columns, 2 * col, 2, 0),
                branch[step][None],
                of_plane(now),
                for_planes(then),
            ]
        ).astype(jnp.int32)
        wide = 2 * TILE
        out = on_core(
            functools.partial(step_kernel, slots_in=slots_in, slots_out=slots_out, blocks=blocks),
            (cols * slots_out * LANES, TILE),
            scratch=(
                pltpu.VMEM((wide, whole), jnp.float32),
                pltpu.VMEM((wide, whole), jnp.bfloat16),
                pltpu.VMEM((wide, whole), jnp.bfloat16),
                pltpu.VMEM((wide, blocks * LANES), jnp.float32),
                pltpu.VMEM((blocks * LANES, whole), jnp.float32),
            ),
        )(info, own, other)
        part = sum_along_col(out.reshape(4, cols // 4, slots_out * LANES, TILE))

    strips = on_core(
        functools.partial(place_kernel, slots=NATURAL, blocks=blocks), (2 * LANES, whole)
    )(of_plane(natural), part, swap_cores(part))
    sharers, height = TILE // LANES, whole // rows
    cut = strips.reshape(2 * LANES, rows // 2, 2, height)
    cut = lax.dynamic_index_in_dim(cut, core, 2, keepdims=False).transpose(1, 0, 2)
    cut = jnp.broadcast_to(cut[:, None], (rows // 2, layers) + cut.shape[1:]).reshape(sharers, 2 * LANES, height)
    back = exchange(cut, ("row", "depth"), plane_groups())
    back = back.reshape(sharers, 2, LANES, height).transpose(1, 0, 2, 3).reshape(2 * TILE, height)
    return back.T


def local(density, pattern, branch):
    rows, cols, layers = lax.axis_size("row"), lax.axis_size("col"), lax.axis_size("depth")
    row, col, layer = lax.axis_index("row"), lax.axis_index("col"), lax.axis_index("depth")
    height, width = density.shape
    blocks = rows * pattern.shape[0]
    cut = density.T.reshape(2, rows // 2, layers, LANES, height)
    cut = lax.dynamic_index_in_dim(cut, layer, 2, keepdims=False).transpose(1, 0, 2, 3)
    cut = cut.reshape(rows // 2, 2 * LANES, height)
    marks = jnp.zeros((LANES, height), jnp.float32).at[:2, : pattern.shape[0]].set(pattern.T.astype(jnp.float32))
    cut = jnp.concatenate([cut, jnp.broadcast_to(marks[None], (rows // 2,) + marks.shape)], axis=1)
    cut = jnp.broadcast_to(cut[:, None], (rows // 2, 2) + cut.shape[1:]).reshape((rows,) + cut.shape[1:])
    got = exchange(cut, "row")
    strips = got[:, : 2 * LANES].transpose(1, 0, 2).reshape(2 * LANES, rows * height)
    marks = got[:, 2 * LANES : 2 * LANES + 2, : pattern.shape[0]].transpose(1, 0, 2).reshape(2, blocks)

    ids = jnp.arange(blocks)
    sent = jnp.zeros((LANES, TILE), jnp.float32).at[:2, :blocks].set(marks)
    seen = gather(sent, "col", cols)[:, :2, :blocks].reshape(blocks, blocks)
    columns = 2 * col + jnp.arange(2)
    held = jnp.where(columns[:, None] == ids, 1, marks.astype(jnp.int32))
    mine = slot_list(held, columns, NATURAL).reshape(2, NATURAL)
    part = on_core(functools.partial(pick_kernel, slots=NATURAL, blocks=blocks), (NATURAL * LANES, TILE))(
        lax.dynamic_index_in_dim(mine, row % 2, 0, keepdims=False), strips
    )
    own, other = in_plane(part)
    keep = jnp.where(ids[:, None] == ids[None, :], 1, seen.astype(jnp.int32))
    order = column_order(keep)
    moved = jnp.dot((order[:, None] == ids).astype(jnp.float32), keep.astype(jnp.float32)).astype(jnp.int32)

    def in_pairs(rows_of):
        return rows_of.reshape((cols, 2) + rows_of.shape[1:])

    natural = slot_list(in_pairs(keep), in_pairs(ids), NATURAL)
    balanced = slot_list(in_pairs(moved), in_pairs(order), BALANCED)
    spare = jnp.stack(
        [2 * NATURAL - in_pairs(keep).sum((1, 2)), 2 * BALANCED - in_pairs(moved).sum((1, 2))]
    )
    return lax.cond(
        spare.min() >= 0,
        lambda: sparse(own, other, natural, balanced, order, branch),
        lambda: dense(density, pattern, branch),
    )


def solution(mesh):
    in_specs = (P("row", "col"), P("row", "col"), P())
    out_specs = P("row", "col")
    return jax.shard_map(local, mesh=mesh, in_specs=in_specs, out_specs=out_specs, check_vma=False)
```

```python
import functools

import jax
import jax.numpy as jnp
from jax import lax
from jax.experimental import pallas as pl
from jax.experimental.pallas import tpu as pltpu
from jax.sharding import PartitionSpec as P

TILE = 128
STEPS = 4
LANES = 8
NATURAL = 18
BALANCED = 14


def exchange(parts, axis, groups=None):
    return lax.all_to_all(parts, axis, 0, 0, axis_index_groups=groups, tiled=True)


def gather(part, axis, members, groups=None):
    return exchange(jnp.broadcast_to(part[None], (members,) + part.shape), axis, groups)


def shifted(parts, by):
    cols = lax.axis_size("col")
    return lax.ppermute(parts, "col", [(z, (z + by) % cols) for z in range(cols)])


def sum_along_col(ahead):
    cols = lax.axis_size("col")
    far = [[c + 4 * m for m in range(cols // 4)] for c in range(4)]
    near = ahead[0] + shifted(ahead[1], 1) + shifted(ahead[3], -1)
    near = near + jnp.concatenate([shifted(ahead[2][:2], 2), shifted(ahead[2][2:], -2)])
    return exchange(near, "col", far).sum(0)


def swap_cores(value):
    return lax.ppermute(value, "row", [(i, i ^ 1) for i in range(lax.axis_size("row"))])


def dense(density, pattern, branch):
    rows, cols = lax.axis_size("row"), lax.axis_size("col")
    layers = lax.axis_size("depth")
    row, col, layer = lax.axis_index("row"), lax.axis_index("col"), lax.axis_index("depth")
    height, width = density.shape
    sub = width // layers
    core = row % 2
    cores_apart = [[x * 2 + c for x in range(rows // 2)] for c in range(2)]

    row_ids = lax.broadcasted_iota(jnp.int32, pattern.shape, 0) + row * pattern.shape[0]
    col_ids = lax.broadcasted_iota(jnp.int32, pattern.shape, 1) + col * pattern.shape[1]
    tiles = jnp.where(row_ids == col_ids, 1, pattern).T.astype(jnp.float32)
    keep = jnp.repeat(jnp.repeat(tiles, TILE, axis=0), TILE, axis=1)
    keep_part = lax.dynamic_slice_in_dim(keep, layer * sub, sub, 0)

    panel = density.T * keep
    part = lax.dynamic_slice_in_dim(panel, layer * sub, sub, 0)
    for step in range(STEPS):
        mine = panel.T.reshape(height // width, layers, sub, width)
        mine = lax.dynamic_index_in_dim(mine, layer, 1, keepdims=False)
        own = gather(mine, "row", rows // 2, cores_apart)
        other = swap_cores(own)

        def product(left, panel=panel):
            out = jnp.dot(
                left.reshape(-1, width), panel, precision=lax.Precision.HIGH, preferred_element_type=jnp.float32
            )
            return out.reshape(rows // 2, 2, sub, height)

        both = jnp.stack([product(own), product(other)])

        def of_class(k, both=both):
            k = k % 4
            start = ((k // 2) ^ core, 0, k % 2, 0, 0)
            out = lax.dynamic_slice(both, start, (1, rows // 2, 1, sub, height))
            return out.reshape(rows // 2, sub, height)

        squared = sum_along_col([of_class(col + q) for q in range(4)])
        part = keep_part * jnp.where(branch[step] == 1, squared, 2.0 * part - squared)
        panel = gather(part, "depth", layers).reshape(width, height)
    return panel.T


def column_order(keep):
    n = keep.shape[0]
    load = keep.sum(0)
    ids = jnp.arange(n)
    ahead = (load[None, :] > load[:, None]) | ((load[None, :] == load[:, None]) & (ids[None, :] < ids[:, None]))
    rank = ahead.astype(jnp.int32).sum(1)
    place = jnp.where(rank < n // 2, 2 * rank, 2 * (n - 1 - rank) + 1)
    return jnp.where(place[None, :] == ids[:, None], ids[None, :], 0).sum(1)


def slot_list(held, columns, slots):
    n = held.shape[-1]
    ids = jnp.arange(n)
    upto = (ids[:, None] <= ids[None, :]).astype(jnp.float32)
    count = jnp.dot(held.astype(jnp.float32), upto).astype(jnp.int32)
    which = jnp.arange(2)[:, None]
    place = count - 1 + which * count[..., :1, -1:]
    value = 1 + 2 * n * (n * columns[..., None] + ids) + n * which + ids
    hit = (held > 0)[..., None] & (place[..., None] == jnp.arange(2 * slots))
    return jnp.where(hit, value[..., None], 0).sum((-3, -2))


def spot(packed, blocks, in_product):
    at = jnp.maximum(packed - 1, 0)
    at = at >> blocks.bit_length() if in_product else at & (2 * blocks - 1)
    return at >> (blocks.bit_length() - 1), pl.ds(pl.multiple_of((at & (blocks - 1)) * TILE, TILE), TILE)


def pick_kernel(info_ref, from_ref, out_ref, *, slots, blocks):
    for t in range(slots):
        block, lanes = spot(info_ref[t], blocks, False)
        rows = pl.ds(pl.multiple_of(block * LANES, LANES), LANES)
        out_ref[t * LANES : (t + 1) * LANES, :] = jnp.where(info_ref[t] > 0, from_ref[rows, lanes], 0.0)


def place_kernel(info_ref, own_ref, other_ref, out_ref, *, slots, blocks):
    out_ref[...] = jnp.zeros_like(out_ref)
    for base, ref in ((0, own_ref), (slots, other_ref)):
        for t in range(slots):
            block, lanes = spot(info_ref[base + t], blocks, False)

            @pl.when(info_ref[base + t] > 0)
            def _(block=block, lanes=lanes, ref=ref, t=t):
                rows = pl.ds(pl.multiple_of(block * LANES, LANES), LANES)
                out_ref[rows, lanes] = ref[t * LANES : (t + 1) * LANES, :]


def step_kernel(info_ref, own_ref, other_ref, out_ref, x_ref, hi_ref, lo_ref, left_ref, prod_ref,
                *, slots_in, slots_out, blocks):
    share, square = info_ref[0], info_ref[3]
    sharers = TILE // LANES
    x_ref[...] = jnp.zeros_like(x_ref)
    for base, ref in ((4, own_ref), (4 + slots_in, other_ref)):

        def place(t, _, base=base, ref=ref):
            block, lanes = spot(info_ref[base + t], blocks, False)

            @pl.when(info_ref[base + t] > 0)
            def _():
                rows = pl.ds(pl.multiple_of(t * LANES, LANES), LANES)
                for s in range(sharers):
                    at = pl.multiple_of(block * TILE + s * LANES, LANES)
                    x_ref[pl.ds(at, LANES), lanes] = ref[s, rows, :]

            return 0

        lax.fori_loop(0, slots_in, place, 0)

    group = lax.broadcasted_iota(jnp.int32, (x_ref.shape[0], TILE), 1) // LANES
    for j in range(blocks):
        lanes = slice(j * TILE, (j + 1) * TILE)
        x = x_ref[:, lanes]
        hi = x.astype(jnp.bfloat16)
        hi_ref[:, lanes] = hi
        lo_ref[:, lanes] = (x - hi.astype(jnp.float32)).astype(jnp.bfloat16)
        half = slice(j // sharers * TILE, (j // sharers + 1) * TILE)
        turned = pltpu.roll(x, ((j - share) & (sharers - 1)) * LANES, 1)
        left_ref[:, half] = jnp.where(group == j % sharers, turned, left_ref[:, half])
    left = left_ref[...].T
    a_hi = left.astype(jnp.bfloat16)
    a_lo = (left - a_hi.astype(jnp.float32)).astype(jnp.bfloat16)
    wide = 4 * TILE
    for j in range(blocks * TILE // wide):
        lanes = slice(j * wide, (j + 1) * wide)
        b_hi, b_lo = hi_ref[:, lanes], lo_ref[:, lanes]
        prod_ref[:, lanes] = (
            jnp.dot(a_hi, b_hi, preferred_element_type=jnp.float32)
            + jnp.dot(a_hi, b_lo, preferred_element_type=jnp.float32)
            + jnp.dot(a_lo, b_hi, preferred_element_type=jnp.float32)
        )

    sign = jnp.where(square == 1, 1.0, -1.0)
    weight = jnp.where(square == 1, 0.0, -2.0)
    for half in range(2):
        rows = pl.ds(pl.multiple_of(info_ref[1 + half] * LANES, LANES), LANES)
        mine = pl.ds(pl.multiple_of(half * TILE + share * LANES, LANES), LANES)
        prod_ref[rows, :] = prod_ref[rows, :] + weight * x_ref[mine, :]

    first = 4 + 2 * slots_in

    def pick(t, _):
        packed = info_ref[first + t]
        block, lanes = spot(packed, blocks, True)
        rows = pl.ds(pl.multiple_of(block * LANES, LANES), LANES)
        out = pl.ds(pl.multiple_of(t * LANES, LANES), LANES)
        out_ref[out, :] = jnp.where(packed > 0, sign * prod_ref[rows, lanes], 0.0)
        return 0

    lax.fori_loop(0, out_ref.shape[0] // LANES, pick, 0, unroll=8)


def on_core(kernel, shape, scratch=()):
    vmem_spec, smem_spec = pl.BlockSpec(memory_space=pltpu.VMEM), pl.BlockSpec(memory_space=pltpu.SMEM)

    def call(info, *arrays):
        return pl.pallas_call(
            kernel,
            out_shape=jax.ShapeDtypeStruct(shape, jnp.float32),
            in_specs=[smem_spec] + [vmem_spec] * len(arrays),
            out_specs=vmem_spec,
            scratch_shapes=list(scratch),
            compiler_params=pltpu.CompilerParams(vmem_limit_bytes=48 * 1024 * 1024),
        )(info, *arrays)

    return call


def plane_groups():
    rows, layers = lax.axis_size("row"), lax.axis_size("depth")
    return [[(x * 2 + c) * layers + y for x in range(rows // 2) for y in range(layers)] for c in range(2)]


def in_plane(part):
    own = gather(part, ("row", "depth"), TILE // LANES, plane_groups())
    return own, swap_cores(own)


def sparse(own, other, natural, balanced, order, branch):
    rows, cols, layers = lax.axis_size("row"), lax.axis_size("col"), lax.axis_size("depth")
    row, col, layer = lax.axis_index("row"), lax.axis_index("col"), lax.axis_index("depth")
    core, share = row % 2, (row // 2) * layers + layer
    blocks = order.shape[0]
    whole = blocks * TILE
    layouts = [(natural, NATURAL, jnp.arange(blocks))] + [(balanced, BALANCED, order)] * (STEPS - 1)
    layouts = layouts + [layouts[0]]

    def of_plane(packed):
        packed = packed.reshape(cols, 2, -1)
        both = lax.dynamic_index_in_dim(packed, col, 0, keepdims=False)
        return jnp.where(core == 0, both, both[::-1]).reshape(-1)

    def for_planes(packed):
        packed = packed.reshape(cols // 4, 4, 2, -1)
        packed = lax.dynamic_index_in_dim(packed, core, 2, keepdims=False)
        twice = jnp.concatenate([packed, packed], axis=1)
        return lax.dynamic_slice_in_dim(twice, col % 4, 4, 1).transpose(1, 0, 2).reshape(-1)

    part = None
    for step in range(STEPS):
        now, slots_in, columns = layouts[step]
        then, slots_out, _ = layouts[step + 1]
        if step > 0:
            own, other = in_plane(part)
        info = jnp.concatenate(
            [
                share[None],
                lax.dynamic_slice_in_dim(columns, 2 * col, 2, 0),
                branch[step][None],
                of_plane(now),
                for_planes(then),
            ]
        ).astype(jnp.int32)
        wide = 2 * TILE
        out = on_core(
            functools.partial(step_kernel, slots_in=slots_in, slots_out=slots_out, blocks=blocks),
            (cols * slots_out * LANES, TILE),
            scratch=(
                pltpu.VMEM((wide, whole), jnp.float32),
                pltpu.VMEM((wide, whole), jnp.bfloat16),
                pltpu.VMEM((wide, whole), jnp.bfloat16),
                pltpu.VMEM((wide, blocks * LANES), jnp.float32),
                pltpu.VMEM((blocks * LANES, whole), jnp.float32),
            ),
        )(info, own, other)
        part = sum_along_col(out.reshape(4, cols // 4, slots_out * LANES, TILE))

    strips = on_core(
        functools.partial(place_kernel, slots=NATURAL, blocks=blocks), (2 * LANES, whole)
    )(of_plane(natural), part, swap_cores(part))
    sharers, height = TILE // LANES, whole // rows
    cut = strips.reshape(2 * LANES, rows // 2, 2, height)
    cut = lax.dynamic_index_in_dim(cut, core, 2, keepdims=False).transpose(1, 0, 2)
    cut = jnp.broadcast_to(cut[:, None], (rows // 2, layers) + cut.shape[1:]).reshape(sharers, 2 * LANES, height)
    back = exchange(cut, ("row", "depth"), plane_groups())
    back = back.reshape(sharers, 2, LANES, height).transpose(1, 0, 2, 3).reshape(2 * TILE, height)
    return back.T


def local(density, pattern, branch):
    rows, cols, layers = lax.axis_size("row"), lax.axis_size("col"), lax.axis_size("depth")
    row, col, layer = lax.axis_index("row"), lax.axis_index("col"), lax.axis_index("depth")
    height, width = density.shape
    blocks = rows * pattern.shape[0]
    cut = density.T.reshape(2, rows // 2, layers, LANES, height)
    cut = lax.dynamic_index_in_dim(cut, layer, 2, keepdims=False).transpose(1, 0, 2, 3)
    cut = cut.reshape(rows // 2, 2 * LANES, height)
    marks = jnp.zeros((LANES, height), jnp.float32).at[:2, : pattern.shape[0]].set(pattern.T.astype(jnp.float32))
    cut = jnp.concatenate([cut, jnp.broadcast_to(marks[None], (rows // 2,) + marks.shape)], axis=1)
    cut = jnp.broadcast_to(cut[:, None], (rows // 2, 2) + cut.shape[1:]).reshape((rows,) + cut.shape[1:])
    got = exchange(cut, "row")
    strips = got[:, : 2 * LANES].transpose(1, 0, 2).reshape(2 * LANES, rows * height)
    marks = got[:, 2 * LANES : 2 * LANES + 2, : pattern.shape[0]].transpose(1, 0, 2).reshape(2, blocks)

    ids = jnp.arange(blocks)
    sent = jnp.zeros((LANES, TILE), jnp.float32).at[:2, :blocks].set(marks)
    seen = lax.all_gather(sent, "col")[:, :2, :blocks].reshape(blocks, blocks)
    columns = 2 * col + jnp.arange(2)
    held = jnp.where(columns[:, None] == ids, 1, marks.astype(jnp.int32))
    mine = slot_list(held, columns, NATURAL).reshape(2, NATURAL)
    part = on_core(functools.partial(pick_kernel, slots=NATURAL, blocks=blocks), (NATURAL * LANES, TILE))(
        lax.dynamic_index_in_dim(mine, row % 2, 0, keepdims=False), strips
    )
    own, other = in_plane(part)
    keep = jnp.where(ids[:, None] == ids[None, :], 1, seen.astype(jnp.int32))
    order = column_order(keep)
    moved = jnp.dot((order[:, None] == ids).astype(jnp.float32), keep.astype(jnp.float32)).astype(jnp.int32)

    def in_pairs(rows_of):
        return rows_of.reshape((cols, 2) + rows_of.shape[1:])

    natural = slot_list(in_pairs(keep), in_pairs(ids), NATURAL)
    balanced = slot_list(in_pairs(moved), in_pairs(order), BALANCED)
    spare = jnp.stack(
        [2 * NATURAL - in_pairs(keep).sum((1, 2)), 2 * BALANCED - in_pairs(moved).sum((1, 2))]
    )
    purified = sparse(own, other, natural, balanced, order, branch)
    return lax.cond(spare.min() >= 0, lambda: purified, lambda: dense(density, pattern, branch))


def solution(mesh):
    in_specs = (P("row", "col"), P("row", "col"), P())
    out_specs = P("row", "col")
    return jax.shard_map(local, mesh=mesh, in_specs=in_specs, out_specs=out_specs, check_vma=False)
```

```python
import functools

import jax
import jax.numpy as jnp
from jax import lax
from jax.experimental import pallas as pl
from jax.experimental.pallas import tpu as pltpu
from jax.sharding import PartitionSpec as P

TILE = 128
STEPS = 4
LANES = 8
NATURAL = 18
BALANCED = 14


def exchange(parts, axis, groups=None):
    return lax.all_to_all(parts, axis, 0, 0, axis_index_groups=groups, tiled=True)


def gather(part, axis, members, groups=None):
    return exchange(jnp.broadcast_to(part[None], (members,) + part.shape), axis, groups)


def shifted(parts, by):
    cols = lax.axis_size("col")
    return lax.ppermute(parts, "col", [(z, (z + by) % cols) for z in range(cols)])


def sum_along_col(ahead):
    cols = lax.axis_size("col")
    far = [[c + 4 * m for m in range(cols // 4)] for c in range(4)]
    near = ahead[0] + shifted(ahead[1], 1) + shifted(ahead[3], -1)
    near = near + jnp.concatenate([shifted(ahead[2][:2], 2), shifted(ahead[2][2:], -2)])
    return exchange(near, "col", far).sum(0)


def sum_slots(own, one, two):
    rows, cols, core = lax.axis_size("row"), lax.axis_size("col"), lax.axis_index("row") % 2
    far = [[c + 4 * m for m in range(cols // 4)] for c in range(4)]

    def apart(value, by):
        steps = [(r, z, (z + by * (1 - 2 * (r % 2))) % cols) for r in range(rows) for z in range(cols)]
        return lax.ppermute(value, ("row", "col"), [(r * cols + z, r * cols + to) for r, z, to in steps])

    one, two = apart(one, 1), apart(two, 2)
    half = lax.broadcasted_iota(jnp.int32, (one.shape[0], 1, 1, 1), 0) // two.shape[0]
    got = one + jnp.where(half == core, jnp.concatenate([two, two]), 0.0)
    theirs = swap_cores(lax.dynamic_index_in_dim(got, 1 - core, 1, keepdims=False))
    near = own + lax.dynamic_index_in_dim(got, core, 1, keepdims=False) + theirs
    return exchange(near, "col", far).sum(0)


def swap_cores(value):
    return lax.ppermute(value, "row", [(i, i ^ 1) for i in range(lax.axis_size("row"))])


def dense(density, pattern, branch):
    rows, cols = lax.axis_size("row"), lax.axis_size("col")
    layers = lax.axis_size("depth")
    row, col, layer = lax.axis_index("row"), lax.axis_index("col"), lax.axis_index("depth")
    height, width = density.shape
    sub = width // layers
    core = row % 2
    cores_apart = [[x * 2 + c for x in range(rows // 2)] for c in range(2)]

    row_ids = lax.broadcasted_iota(jnp.int32, pattern.shape, 0) + row * pattern.shape[0]
    col_ids = lax.broadcasted_iota(jnp.int32, pattern.shape, 1) + col * pattern.shape[1]
    tiles = jnp.where(row_ids == col_ids, 1, pattern).T.astype(jnp.float32)
    keep = jnp.repeat(jnp.repeat(tiles, TILE, axis=0), TILE, axis=1)
    keep_part = lax.dynamic_slice_in_dim(keep, layer * sub, sub, 0)

    panel = density.T * keep
    part = lax.dynamic_slice_in_dim(panel, layer * sub, sub, 0)
    for step in range(STEPS):
        mine = panel.T.reshape(height // width, layers, sub, width)
        mine = lax.dynamic_index_in_dim(mine, layer, 1, keepdims=False)
        own = gather(mine, "row", rows // 2, cores_apart)
        other = swap_cores(own)

        def product(left, panel=panel):
            out = jnp.dot(
                left.reshape(-1, width), panel, precision=lax.Precision.HIGH, preferred_element_type=jnp.float32
            )
            return out.reshape(rows // 2, 2, sub, height)

        both = jnp.stack([product(own), product(other)])

        def of_class(k, both=both):
            k = k % 4
            start = ((k // 2) ^ core, 0, k % 2, 0, 0)
            out = lax.dynamic_slice(both, start, (1, rows // 2, 1, sub, height))
            return out.reshape(rows // 2, sub, height)

        squared = sum_along_col([of_class(col + q) for q in range(4)])
        part = keep_part * jnp.where(branch[step] == 1, squared, 2.0 * part - squared)
        panel = gather(part, "depth", layers).reshape(width, height)
    return panel.T


def column_order(keep):
    n = keep.shape[0]
    load = keep.sum(0)
    ids = jnp.arange(n)
    ahead = (load[None, :] > load[:, None]) | ((load[None, :] == load[:, None]) & (ids[None, :] < ids[:, None]))
    rank = ahead.astype(jnp.int32).sum(1)
    place = jnp.where(rank < n // 2, 2 * rank, 2 * (n - 1 - rank) + 1)
    return jnp.where(place[None, :] == ids[:, None], ids[None, :], 0).sum(1)


def slot_list(held, columns, slots):
    n = held.shape[-1]
    ids = jnp.arange(n)
    upto = (ids[:, None] <= ids[None, :]).astype(jnp.float32)
    count = jnp.dot(held.astype(jnp.float32), upto).astype(jnp.int32)
    which = jnp.arange(2)[:, None]
    place = count - 1 + which * count[..., :1, -1:]
    value = 1 + 2 * n * (n * columns[..., None] + ids) + n * which + ids
    hit = (held > 0)[..., None] & (place[..., None] == jnp.arange(2 * slots))
    return jnp.where(hit, value[..., None], 0).sum((-3, -2))


def spot(packed, blocks, in_product):
    at = jnp.maximum(packed - 1, 0)
    at = at >> blocks.bit_length() if in_product else at & (2 * blocks - 1)
    return at >> (blocks.bit_length() - 1), pl.ds(pl.multiple_of((at & (blocks - 1)) * TILE, TILE), TILE)


def pick_kernel(info_ref, from_ref, out_ref, *, slots, blocks):
    for t in range(slots):
        block, lanes = spot(info_ref[t], blocks, False)
        rows = pl.ds(pl.multiple_of(block * LANES, LANES), LANES)
        out_ref[t * LANES : (t + 1) * LANES, :] = jnp.where(info_ref[t] > 0, from_ref[rows, lanes], 0.0)


def place_kernel(info_ref, own_ref, other_ref, out_ref, *, slots, blocks):
    out_ref[...] = jnp.zeros_like(out_ref)
    for base, ref in ((0, own_ref), (slots, other_ref)):
        for t in range(slots):
            block, lanes = spot(info_ref[base + t], blocks, False)

            @pl.when(info_ref[base + t] > 0)
            def _(block=block, lanes=lanes, ref=ref, t=t):
                rows = pl.ds(pl.multiple_of(block * LANES, LANES), LANES)
                out_ref[rows, lanes] = ref[t * LANES : (t + 1) * LANES, :]


def step_kernel(info_ref, own_ref, other_ref, out_ref, x_ref, hi_ref, lo_ref, left_ref, prod_ref,
                *, slots_in, slots_out, blocks):
    share, square = info_ref[0], info_ref[3]
    sharers = TILE // LANES
    x_ref[...] = jnp.zeros_like(x_ref)
    for base, ref in ((4, own_ref), (4 + slots_in, other_ref)):

        def place(t, _, base=base, ref=ref):
            block, lanes = spot(info_ref[base + t], blocks, False)

            @pl.when(info_ref[base + t] > 0)
            def _():
                rows = pl.ds(pl.multiple_of(t * LANES, LANES), LANES)
                for s in range(sharers):
                    at = pl.multiple_of(block * TILE + s * LANES, LANES)
                    x_ref[pl.ds(at, LANES), lanes] = ref[s, rows, :]

            return 0

        lax.fori_loop(0, slots_in, place, 0)

    group = lax.broadcasted_iota(jnp.int32, (x_ref.shape[0], TILE), 1) // LANES
    for j in range(blocks):
        lanes = slice(j * TILE, (j + 1) * TILE)
        x = x_ref[:, lanes]
        hi = x.astype(jnp.bfloat16)
        hi_ref[:, lanes] = hi
        lo_ref[:, lanes] = (x - hi.astype(jnp.float32)).astype(jnp.bfloat16)
        half = slice(j // sharers * TILE, (j // sharers + 1) * TILE)
        turned = pltpu.roll(x, ((j - share) & (sharers - 1)) * LANES, 1)
        left_ref[:, half] = jnp.where(group == j % sharers, turned, left_ref[:, half])
    left = left_ref[...].T
    a_hi = left.astype(jnp.bfloat16)
    a_lo = (left - a_hi.astype(jnp.float32)).astype(jnp.bfloat16)
    wide = 4 * TILE
    for j in range(blocks * TILE // wide):
        lanes = slice(j * wide, (j + 1) * wide)
        b_hi, b_lo = hi_ref[:, lanes], lo_ref[:, lanes]
        prod_ref[:, lanes] = (
            jnp.dot(a_hi, b_hi, preferred_element_type=jnp.float32)
            + jnp.dot(a_hi, b_lo, preferred_element_type=jnp.float32)
            + jnp.dot(a_lo, b_hi, preferred_element_type=jnp.float32)
        )

    sign = jnp.where(square == 1, 1.0, -1.0)
    weight = jnp.where(square == 1, 0.0, -2.0)
    for half in range(2):
        rows = pl.ds(pl.multiple_of(info_ref[1 + half] * LANES, LANES), LANES)
        mine = pl.ds(pl.multiple_of(half * TILE + share * LANES, LANES), LANES)
        prod_ref[rows, :] = prod_ref[rows, :] + weight * x_ref[mine, :]

    first = 4 + 2 * slots_in

    def pick(t, _):
        packed = info_ref[first + t]
        block, lanes = spot(packed, blocks, True)
        rows = pl.ds(pl.multiple_of(block * LANES, LANES), LANES)
        out = pl.ds(pl.multiple_of(t * LANES, LANES), LANES)
        out_ref[out, :] = jnp.where(packed > 0, sign * prod_ref[rows, lanes], 0.0)
        return 0

    lax.fori_loop(0, out_ref.shape[0] // LANES, pick, 0, unroll=8)


def on_core(kernel, shape, scratch=()):
    vmem_spec, smem_spec = pl.BlockSpec(memory_space=pltpu.VMEM), pl.BlockSpec(memory_space=pltpu.SMEM)

    def call(info, *arrays):
        return pl.pallas_call(
            kernel,
            out_shape=jax.ShapeDtypeStruct(shape, jnp.float32),
            in_specs=[smem_spec] + [vmem_spec] * len(arrays),
            out_specs=vmem_spec,
            scratch_shapes=list(scratch),
            compiler_params=pltpu.CompilerParams(vmem_limit_bytes=48 * 1024 * 1024),
        )(info, *arrays)

    return call


def plane_groups():
    rows, layers = lax.axis_size("row"), lax.axis_size("depth")
    return [[(x * 2 + c) * layers + y for x in range(rows // 2) for y in range(layers)] for c in range(2)]


def in_plane(part):
    own = gather(part, ("row", "depth"), TILE // LANES, plane_groups())
    return own, swap_cores(own)


def sparse(own, other, natural, balanced, order, branch):
    rows, cols, layers = lax.axis_size("row"), lax.axis_size("col"), lax.axis_size("depth")
    row, col, layer = lax.axis_index("row"), lax.axis_index("col"), lax.axis_index("depth")
    core, share = row % 2, (row // 2) * layers + layer
    blocks = order.shape[0]
    whole = blocks * TILE
    layouts = [(natural, NATURAL, jnp.arange(blocks))] + [(balanced, BALANCED, order)] * (STEPS - 1)
    layouts = layouts + [layouts[0]]

    def of_plane(packed):
        packed = packed.reshape(cols, 2, -1)
        both = lax.dynamic_index_in_dim(packed, col, 0, keepdims=False)
        return jnp.where(core == 0, both, both[::-1]).reshape(-1)

    def for_planes(packed):
        packed = packed.reshape(cols // 4, 4, -1)
        slots = packed.shape[2] // 2

        def of_class(by):
            return lax.dynamic_index_in_dim(packed, (col + by) % 4, 1, keepdims=False)

        own = lax.dynamic_slice_in_dim(of_class(0), core * slots, slots, 1)
        two = lax.dynamic_slice_in_dim(of_class(2), core * (cols // 8), cols // 8, 0)
        return jnp.concatenate([v.reshape(-1) for v in (own, of_class(1 + 2 * core), two)])

    part = None
    for step in range(STEPS):
        now, slots_in, columns = layouts[step]
        then, slots_out, _ = layouts[step + 1]
        if step > 0:
            own, other = in_plane(part)
        info = jnp.concatenate(
            [
                share[None],
                lax.dynamic_slice_in_dim(columns, 2 * col, 2, 0),
                branch[step][None],
                of_plane(now),
                for_planes(then),
            ]
        ).astype(jnp.int32)
        wide = 2 * TILE
        out = on_core(
            functools.partial(step_kernel, slots_in=slots_in, slots_out=slots_out, blocks=blocks),
            (cols * slots_out * LANES, TILE),
            scratch=(
                pltpu.VMEM((wide, whole), jnp.float32),
                pltpu.VMEM((wide, whole), jnp.bfloat16),
                pltpu.VMEM((wide, whole), jnp.bfloat16),
                pltpu.VMEM((wide, blocks * LANES), jnp.float32),
                pltpu.VMEM((blocks * LANES, whole), jnp.float32),
            ),
        )(info, own, other)
        quads, tall = cols // 4, slots_out * LANES
        own, one, two = jnp.split(out, [quads * tall, 3 * quads * tall])
        part = sum_slots(
            own.reshape(quads, tall, TILE), one.reshape(quads, 2, tall, TILE), two.reshape(-1, 2, tall, TILE)
        )

    strips = on_core(
        functools.partial(place_kernel, slots=NATURAL, blocks=blocks), (2 * LANES, whole)
    )(of_plane(natural), part, swap_cores(part))
    sharers, height = TILE // LANES, whole // rows
    cut = strips.reshape(2 * LANES, rows // 2, 2, height)
    cut = lax.dynamic_index_in_dim(cut, core, 2, keepdims=False).transpose(1, 0, 2)
    cut = jnp.broadcast_to(cut[:, None], (rows // 2, layers) + cut.shape[1:]).reshape(sharers, 2 * LANES, height)
    back = exchange(cut, ("row", "depth"), plane_groups())
    back = back.reshape(sharers, 2, LANES, height).transpose(1, 0, 2, 3).reshape(2 * TILE, height)
    return back.T


def local(density, pattern, branch):
    rows, cols, layers = lax.axis_size("row"), lax.axis_size("col"), lax.axis_size("depth")
    row, col, layer = lax.axis_index("row"), lax.axis_index("col"), lax.axis_index("depth")
    height, width = density.shape
    blocks = rows * pattern.shape[0]
    cut = density.T.reshape(2, rows // 2, layers, LANES, height)
    cut = lax.dynamic_index_in_dim(cut, layer, 2, keepdims=False).transpose(1, 0, 2, 3)
    cut = cut.reshape(rows // 2, 2 * LANES, height)
    marks = jnp.zeros((LANES, height), jnp.float32).at[:2, : pattern.shape[0]].set(pattern.T.astype(jnp.float32))
    cut = jnp.concatenate([cut, jnp.broadcast_to(marks[None], (rows // 2,) + marks.shape)], axis=1)
    cut = jnp.broadcast_to(cut[:, None], (rows // 2, 2) + cut.shape[1:]).reshape((rows,) + cut.shape[1:])
    got = exchange(cut, "row")
    strips = got[:, : 2 * LANES].transpose(1, 0, 2).reshape(2 * LANES, rows * height)
    marks = got[:, 2 * LANES : 2 * LANES + 2, : pattern.shape[0]].transpose(1, 0, 2).reshape(2, blocks)

    ids = jnp.arange(blocks)
    sent = jnp.zeros((LANES, TILE), jnp.float32).at[:2, :blocks].set(marks)
    seen = lax.all_gather(sent, "col")[:, :2, :blocks].reshape(blocks, blocks)
    columns = 2 * col + jnp.arange(2)
    held = jnp.where(columns[:, None] == ids, 1, marks.astype(jnp.int32))
    mine = slot_list(held, columns, NATURAL).reshape(2, NATURAL)
    part = on_core(functools.partial(pick_kernel, slots=NATURAL, blocks=blocks), (NATURAL * LANES, TILE))(
        lax.dynamic_index_in_dim(mine, row % 2, 0, keepdims=False), strips
    )
    own, other = in_plane(part)
    keep = jnp.where(ids[:, None] == ids[None, :], 1, seen.astype(jnp.int32))
    order = column_order(keep)
    moved = jnp.dot((order[:, None] == ids).astype(jnp.float32), keep.astype(jnp.float32)).astype(jnp.int32)

    def in_pairs(rows_of):
        return rows_of.reshape((cols, 2) + rows_of.shape[1:])

    natural = slot_list(in_pairs(keep), in_pairs(ids), NATURAL)
    balanced = slot_list(in_pairs(moved), in_pairs(order), BALANCED)
    spare = jnp.stack(
        [2 * NATURAL - in_pairs(keep).sum((1, 2)), 2 * BALANCED - in_pairs(moved).sum((1, 2))]
    )
    purified = sparse(own, other, natural, balanced, order, branch)
    return lax.cond(spare.min() >= 0, lambda: purified, lambda: dense(density, pattern, branch))


def solution(mesh):
    in_specs = (P("row", "col"), P("row", "col"), P())
    out_specs = P("row", "col")
    return jax.shard_map(local, mesh=mesh, in_specs=in_specs, out_specs=out_specs, check_vma=False)
```

```python
import functools

import jax
import jax.numpy as jnp
from jax import lax
from jax.experimental import pallas as pl
from jax.experimental.pallas import tpu as pltpu
from jax.sharding import PartitionSpec as P

TILE = 128
STEPS = 4
LANES = 8
NATURAL = 18
BALANCED = 14


def exchange(parts, axis, groups=None):
    return lax.all_to_all(parts, axis, 0, 0, axis_index_groups=groups, tiled=True)


def gather(part, axis, members, groups=None):
    return exchange(jnp.broadcast_to(part[None], (members,) + part.shape), axis, groups)


def shifted(parts, by):
    cols = lax.axis_size("col")
    return lax.ppermute(parts, "col", [(z, (z + by) % cols) for z in range(cols)])


def sum_along_col(ahead):
    cols = lax.axis_size("col")
    far = [[c + 4 * m for m in range(cols // 4)] for c in range(4)]
    near = ahead[0] + shifted(ahead[1], 1) + shifted(ahead[3], -1)
    near = near + jnp.concatenate([shifted(ahead[2][:2], 2), shifted(ahead[2][2:], -2)])
    return exchange(near, "col", far).sum(0)


def swap_cores(value):
    return lax.ppermute(value, "row", [(i, i ^ 1) for i in range(lax.axis_size("row"))])


def dense(density, pattern, branch):
    rows, cols = lax.axis_size("row"), lax.axis_size("col")
    layers = lax.axis_size("depth")
    row, col, layer = lax.axis_index("row"), lax.axis_index("col"), lax.axis_index("depth")
    height, width = density.shape
    sub = width // layers
    core = row % 2
    cores_apart = [[x * 2 + c for x in range(rows // 2)] for c in range(2)]

    row_ids = lax.broadcasted_iota(jnp.int32, pattern.shape, 0) + row * pattern.shape[0]
    col_ids = lax.broadcasted_iota(jnp.int32, pattern.shape, 1) + col * pattern.shape[1]
    tiles = jnp.where(row_ids == col_ids, 1, pattern).T.astype(jnp.float32)
    keep = jnp.repeat(jnp.repeat(tiles, TILE, axis=0), TILE, axis=1)
    keep_part = lax.dynamic_slice_in_dim(keep, layer * sub, sub, 0)

    panel = density.T * keep
    part = lax.dynamic_slice_in_dim(panel, layer * sub, sub, 0)
    for step in range(STEPS):
        mine = panel.T.reshape(height // width, layers, sub, width)
        mine = lax.dynamic_index_in_dim(mine, layer, 1, keepdims=False)
        own = gather(mine, "row", rows // 2, cores_apart)
        other = swap_cores(own)

        def product(left, panel=panel):
            out = jnp.dot(
                left.reshape(-1, width), panel, precision=lax.Precision.HIGH, preferred_element_type=jnp.float32
            )
            return out.reshape(rows // 2, 2, sub, height)

        both = jnp.stack([product(own), product(other)])

        def of_class(k, both=both):
            k = k % 4
            start = ((k // 2) ^ core, 0, k % 2, 0, 0)
            out = lax.dynamic_slice(both, start, (1, rows // 2, 1, sub, height))
            return out.reshape(rows // 2, sub, height)

        squared = sum_along_col([of_class(col + q) for q in range(4)])
        part = keep_part * jnp.where(branch[step] == 1, squared, 2.0 * part - squared)
        panel = gather(part, "depth", layers).reshape(width, height)
    return panel.T


def column_order(keep):
    n = keep.shape[0]
    load = keep.sum(0)
    ids = jnp.arange(n)
    ahead = (load[None, :] > load[:, None]) | ((load[None, :] == load[:, None]) & (ids[None, :] < ids[:, None]))
    rank = ahead.astype(jnp.int32).sum(1)
    place = jnp.where(rank < n // 2, 2 * rank, 2 * (n - 1 - rank) + 1)
    return jnp.where(place[None, :] == ids[:, None], ids[None, :], 0).sum(1)


def slot_list(held, columns, slots):
    n = held.shape[-1]
    ids = jnp.arange(n)
    upto = (ids[:, None] <= ids[None, :]).astype(jnp.float32)
    count = jnp.dot(held.astype(jnp.float32), upto).astype(jnp.int32)
    which = jnp.arange(2)[:, None]
    place = count - 1 + which * count[..., :1, -1:]
    value = 1 + 2 * n * (n * columns[..., None] + ids) + n * which + ids
    hit = (held > 0)[..., None] & (place[..., None] == jnp.arange(2 * slots))
    return jnp.where(hit, value[..., None], 0).sum((-3, -2))


def spot(packed, blocks, in_product):
    at = jnp.maximum(packed - 1, 0)
    at = at >> blocks.bit_length() if in_product else at & (2 * blocks - 1)
    return at >> (blocks.bit_length() - 1), pl.ds(pl.multiple_of((at & (blocks - 1)) * TILE, TILE), TILE)


def pick_kernel(info_ref, from_ref, out_ref, *, slots, blocks):
    for t in range(slots):
        block, lanes = spot(info_ref[t], blocks, False)
        rows = pl.ds(pl.multiple_of(block * LANES, LANES), LANES)
        out_ref[t * LANES : (t + 1) * LANES, :] = jnp.where(info_ref[t] > 0, from_ref[rows, lanes], 0.0)


def place_kernel(info_ref, own_ref, other_ref, out_ref, *, slots, blocks):
    out_ref[...] = jnp.zeros_like(out_ref)
    for base, ref in ((0, own_ref), (slots, other_ref)):
        for t in range(slots):
            block, lanes = spot(info_ref[base + t], blocks, False)

            @pl.when(info_ref[base + t] > 0)
            def _(block=block, lanes=lanes, ref=ref, t=t):
                rows = pl.ds(pl.multiple_of(block * LANES, LANES), LANES)
                out_ref[rows, lanes] = ref[t * LANES : (t + 1) * LANES, :]


def step_kernel(info_ref, own_ref, other_ref, out_ref, x_ref, hi_ref, lo_ref, left_ref, prod_ref,
                *, slots_in, slots_out, blocks):
    share, square = info_ref[0], info_ref[3]
    sharers = TILE // LANES
    x_ref[...] = jnp.zeros_like(x_ref)
    for base, ref in ((4, own_ref), (4 + slots_in, other_ref)):

        def place(t, _, base=base, ref=ref):
            block, lanes = spot(info_ref[base + t], blocks, False)

            @pl.when(info_ref[base + t] > 0)
            def _():
                rows = pl.ds(pl.multiple_of(t * LANES, LANES), LANES)
                for s in range(sharers):
                    at = pl.multiple_of(block * TILE + s * LANES, LANES)
                    x_ref[pl.ds(at, LANES), lanes] = ref[s, rows, :]

            return 0

        lax.fori_loop(0, slots_in, place, 0)

    group = lax.broadcasted_iota(jnp.int32, (x_ref.shape[0], TILE), 1) // LANES
    for j in range(blocks):
        lanes = slice(j * TILE, (j + 1) * TILE)
        x = x_ref[:, lanes]
        hi = x.astype(jnp.bfloat16)
        hi_ref[:, lanes] = hi
        lo_ref[:, lanes] = (x - hi.astype(jnp.float32)).astype(jnp.bfloat16)
        half = slice(j // sharers * TILE, (j // sharers + 1) * TILE)
        turned = pltpu.roll(x, ((j - share) & (sharers - 1)) * LANES, 1)
        left_ref[:, half] = jnp.where(group == j % sharers, turned, left_ref[:, half])
    left = left_ref[...].T
    a_hi = left.astype(jnp.bfloat16)
    a_lo = (left - a_hi.astype(jnp.float32)).astype(jnp.bfloat16)
    wide = 4 * TILE
    for j in range(blocks * TILE // wide):
        lanes = slice(j * wide, (j + 1) * wide)
        b_hi, b_lo = hi_ref[:, lanes], lo_ref[:, lanes]
        prod_ref[:, lanes] = (
            jnp.dot(a_hi, b_hi, preferred_element_type=jnp.float32)
            + jnp.dot(a_hi, b_lo, preferred_element_type=jnp.float32)
            + jnp.dot(a_lo, b_hi, preferred_element_type=jnp.float32)
        )

    sign = jnp.where(square == 1, 1.0, -1.0)
    weight = jnp.where(square == 1, 0.0, -2.0)
    for half in range(2):
        rows = pl.ds(pl.multiple_of(info_ref[1 + half] * LANES, LANES), LANES)
        mine = pl.ds(pl.multiple_of(half * TILE + share * LANES, LANES), LANES)
        prod_ref[rows, :] = prod_ref[rows, :] + weight * x_ref[mine, :]

    first = 4 + 2 * slots_in

    def pick(t, _):
        packed = info_ref[first + t]
        block, lanes = spot(packed, blocks, True)
        rows = pl.ds(pl.multiple_of(block * LANES, LANES), LANES)
        out = pl.ds(pl.multiple_of(t * LANES, LANES), LANES)
        out_ref[out, :] = jnp.where(packed > 0, sign * prod_ref[rows, lanes], 0.0)
        return 0

    lax.fori_loop(0, out_ref.shape[0] // LANES, pick, 0, unroll=8)


def on_core(kernel, shape, scratch=()):
    vmem_spec, smem_spec = pl.BlockSpec(memory_space=pltpu.VMEM), pl.BlockSpec(memory_space=pltpu.SMEM)

    def call(info, *arrays):
        return pl.pallas_call(
            kernel,
            out_shape=jax.ShapeDtypeStruct(shape, jnp.float32),
            in_specs=[smem_spec] + [vmem_spec] * len(arrays),
            out_specs=vmem_spec,
            scratch_shapes=list(scratch),
            compiler_params=pltpu.CompilerParams(vmem_limit_bytes=48 * 1024 * 1024),
        )(info, *arrays)

    return call


def plane_groups():
    rows, layers = lax.axis_size("row"), lax.axis_size("depth")
    return [[(x * 2 + c) * layers + y for x in range(rows // 2) for y in range(layers)] for c in range(2)]


def in_plane(part):
    own = gather(part, ("row", "depth"), TILE // LANES, plane_groups())
    return own, swap_cores(own)


def sparse(own, other, natural, balanced, order, branch):
    rows, cols, layers = lax.axis_size("row"), lax.axis_size("col"), lax.axis_size("depth")
    row, col, layer = lax.axis_index("row"), lax.axis_index("col"), lax.axis_index("depth")
    core, share = row % 2, (row // 2) * layers + layer
    blocks = order.shape[0]
    whole = blocks * TILE
    layouts = [(natural, NATURAL, jnp.arange(blocks))] + [(balanced, BALANCED, order)] * (STEPS - 1)
    layouts = layouts + [layouts[0]]

    def of_plane(packed):
        packed = packed.reshape(cols, 2, -1)
        both = lax.dynamic_index_in_dim(packed, col, 0, keepdims=False)
        return jnp.where(core == 0, both, both[::-1]).reshape(-1)

    def for_planes(packed):
        packed = packed.reshape(cols // 4, 4, 2, -1)
        packed = lax.dynamic_index_in_dim(packed, core, 2, keepdims=False)
        twice = jnp.concatenate([packed, packed], axis=1)
        return lax.dynamic_slice_in_dim(twice, col % 4, 4, 1).transpose(1, 0, 2).reshape(-1)

    part = None
    for step in range(STEPS):
        now, slots_in, columns = layouts[step]
        then, slots_out, _ = layouts[step + 1]
        if step > 0:
            own, other = in_plane(part)
        info = jnp.concatenate(
            [
                share[None],
                lax.dynamic_slice_in_dim(columns, 2 * col, 2, 0),
                branch[step][None],
                of_plane(now),
                for_planes(then),
            ]
        ).astype(jnp.int32)
        wide = 2 * TILE
        out = on_core(
            functools.partial(step_kernel, slots_in=slots_in, slots_out=slots_out, blocks=blocks),
            (cols * slots_out * LANES, TILE),
            scratch=(
                pltpu.VMEM((wide, whole), jnp.float32),
                pltpu.VMEM((wide, whole), jnp.bfloat16),
                pltpu.VMEM((wide, whole), jnp.bfloat16),
                pltpu.VMEM((wide, blocks * LANES), jnp.float32),
                pltpu.VMEM((blocks * LANES, whole), jnp.float32),
            ),
        )(info, own, other)
        part = sum_along_col(out.reshape(4, cols // 4, slots_out * LANES, TILE))

    strips = on_core(
        functools.partial(place_kernel, slots=NATURAL, blocks=blocks), (2 * LANES, whole)
    )(of_plane(natural), part, swap_cores(part))
    sharers, height = TILE // LANES, whole // rows
    cut = strips.reshape(2 * LANES, rows // 2, 2, height)
    cut = lax.dynamic_index_in_dim(cut, core, 2, keepdims=False).transpose(1, 0, 2)
    cut = jnp.broadcast_to(cut[:, None], (rows // 2, layers) + cut.shape[1:]).reshape(sharers, 2 * LANES, height)
    back = exchange(cut, ("row", "depth"), plane_groups())
    back = back.reshape(sharers, 2, LANES, height).transpose(1, 0, 2, 3).reshape(2 * TILE, height)
    return back.T


def local(density, pattern, branch):
    rows, cols, layers = lax.axis_size("row"), lax.axis_size("col"), lax.axis_size("depth")
    row, col, layer = lax.axis_index("row"), lax.axis_index("col"), lax.axis_index("depth")
    height, width = density.shape
    blocks = rows * pattern.shape[0]
    cut = density.T.reshape(2, rows // 2, layers, LANES, height)
    cut = lax.dynamic_index_in_dim(cut, layer, 2, keepdims=False).transpose(1, 0, 2, 3)
    cut = cut.reshape(rows // 2, 2 * LANES, height)
    marks = jnp.zeros((LANES, height), jnp.float32).at[:2, : pattern.shape[0]].set(pattern.T.astype(jnp.float32))
    cut = jnp.concatenate([cut, jnp.broadcast_to(marks[None], (rows // 2,) + marks.shape)], axis=1)
    cut = jnp.broadcast_to(cut[:, None], (rows // 2, 2) + cut.shape[1:]).reshape((rows,) + cut.shape[1:])
    got = exchange(cut, "row")
    strips = got[:, : 2 * LANES].transpose(1, 0, 2).reshape(2 * LANES, rows * height)
    marks = got[:, 2 * LANES : 2 * LANES + 2, : pattern.shape[0]].transpose(1, 0, 2).reshape(2, blocks)

    ids = jnp.arange(blocks)
    sent = jnp.zeros((LANES, TILE), jnp.float32).at[:2, :blocks].set(marks)
    steps = [(r, z, y, (z - r // 2 * layers - y) % cols) for r in range(rows) for z in range(cols) for y in range(layers)]
    ahead = lax.ppermute(
        sent,
        ("row", "col", "depth"),
        [((r * cols + z) * layers + y, (r * cols + to) * layers + y) for r, z, y, to in steps],
    )
    columns = 2 * col + jnp.arange(2)
    held = jnp.where(columns[:, None] == ids, 1, marks.astype(jnp.int32))
    mine = slot_list(held, columns, NATURAL).reshape(2, NATURAL)
    part = on_core(functools.partial(pick_kernel, slots=NATURAL, blocks=blocks), (NATURAL * LANES, TILE))(
        lax.dynamic_index_in_dim(mine, row % 2, 0, keepdims=False), strips
    )
    own, other = in_plane(jnp.concatenate([part, ahead]))
    seen = own[:, NATURAL * LANES : NATURAL * LANES + 2, :blocks].reshape(2 * cols, blocks)
    seen = lax.dynamic_slice_in_dim(jnp.concatenate([seen, seen]), 2 * (cols - col), 2 * cols, 0)
    keep = jnp.where(ids[:, None] == ids[None, :], 1, seen.astype(jnp.int32))
    order = column_order(keep)
    moved = jnp.dot((order[:, None] == ids).astype(jnp.float32), keep.astype(jnp.float32)).astype(jnp.int32)

    def in_pairs(rows_of):
        return rows_of.reshape((cols, 2) + rows_of.shape[1:])

    natural = slot_list(in_pairs(keep), in_pairs(ids), NATURAL)
    balanced = slot_list(in_pairs(moved), in_pairs(order), BALANCED)
    spare = jnp.stack(
        [2 * NATURAL - in_pairs(keep).sum((1, 2)), 2 * BALANCED - in_pairs(moved).sum((1, 2))]
    )
    purified = sparse(own, other, natural, balanced, order, branch)
    return lax.cond(spare.min() >= 0, lambda: purified, lambda: dense(density, pattern, branch))


def solution(mesh):
    in_specs = (P("row", "col"), P("row", "col"), P())
    out_specs = P("row", "col")
    return jax.shard_map(local, mesh=mesh, in_specs=in_specs, out_specs=out_specs, check_vma=False)
```

```python
import functools

import jax
import jax.numpy as jnp
from jax import lax
from jax.experimental import pallas as pl
from jax.experimental.pallas import tpu as pltpu
from jax.sharding import PartitionSpec as P

TILE = 128
STEPS = 4
LANES = 8
NATURAL = 18
BALANCED = 14


def exchange(parts, axis, groups=None):
    return lax.all_to_all(parts, axis, 0, 0, axis_index_groups=groups, tiled=True)


def gather(part, axis, members, groups=None):
    return exchange(jnp.broadcast_to(part[None], (members,) + part.shape), axis, groups)


def shifted(parts, by):
    cols = lax.axis_size("col")
    return lax.ppermute(parts, "col", [(z, (z + by) % cols) for z in range(cols)])


def sum_along_col(ahead):
    cols = lax.axis_size("col")
    far = [[c + 4 * m for m in range(cols // 4)] for c in range(4)]
    near = ahead[0] + shifted(ahead[1], 1) + shifted(ahead[3], -1)
    near = near + jnp.concatenate([shifted(ahead[2][:2], 2), shifted(ahead[2][2:], -2)])
    return exchange(near, "col", far).sum(0)


def swap_cores(value):
    return lax.ppermute(value, "row", [(i, i ^ 1) for i in range(lax.axis_size("row"))])


def dense(density, pattern, branch):
    rows, cols = lax.axis_size("row"), lax.axis_size("col")
    layers = lax.axis_size("depth")
    row, col, layer = lax.axis_index("row"), lax.axis_index("col"), lax.axis_index("depth")
    height, width = density.shape
    sub = width // layers
    core = row % 2
    cores_apart = [[x * 2 + c for x in range(rows // 2)] for c in range(2)]

    row_ids = lax.broadcasted_iota(jnp.int32, pattern.shape, 0) + row * pattern.shape[0]
    col_ids = lax.broadcasted_iota(jnp.int32, pattern.shape, 1) + col * pattern.shape[1]
    tiles = jnp.where(row_ids == col_ids, 1, pattern).T.astype(jnp.float32)
    keep = jnp.repeat(jnp.repeat(tiles, TILE, axis=0), TILE, axis=1)
    keep_part = lax.dynamic_slice_in_dim(keep, layer * sub, sub, 0)

    panel = density.T * keep
    part = lax.dynamic_slice_in_dim(panel, layer * sub, sub, 0)
    for step in range(STEPS):
        mine = panel.T.reshape(height // width, layers, sub, width)
        mine = lax.dynamic_index_in_dim(mine, layer, 1, keepdims=False)
        own = gather(mine, "row", rows // 2, cores_apart)
        other = swap_cores(own)

        def product(left, panel=panel):
            out = jnp.dot(
                left.reshape(-1, width), panel, precision=lax.Precision.HIGH, preferred_element_type=jnp.float32
            )
            return out.reshape(rows // 2, 2, sub, height)

        both = jnp.stack([product(own), product(other)])

        def of_class(k, both=both):
            k = k % 4
            start = ((k // 2) ^ core, 0, k % 2, 0, 0)
            out = lax.dynamic_slice(both, start, (1, rows // 2, 1, sub, height))
            return out.reshape(rows // 2, sub, height)

        squared = sum_along_col([of_class(col + q) for q in range(4)])
        part = keep_part * jnp.where(branch[step] == 1, squared, 2.0 * part - squared)
        panel = gather(part, "depth", layers).reshape(width, height)
    return panel.T


def column_order(keep):
    n = keep.shape[0]
    load = keep.sum(0)
    ids = jnp.arange(n)
    ahead = (load[None, :] > load[:, None]) | ((load[None, :] == load[:, None]) & (ids[None, :] < ids[:, None]))
    rank = ahead.astype(jnp.int32).sum(1)
    place = jnp.where(rank < n // 2, 2 * rank, 2 * (n - 1 - rank) + 1)
    return jnp.where(place[None, :] == ids[:, None], ids[None, :], 0).sum(1)


def slot_list(held, columns, slots):
    n = held.shape[-1]
    ids = jnp.arange(n)
    upto = (ids[:, None] <= ids[None, :]).astype(jnp.float32)
    count = jnp.dot(held.astype(jnp.float32), upto).astype(jnp.int32)
    which = jnp.arange(2)[:, None]
    place = count - 1 + which * count[..., :1, -1:]
    value = 1 + 2 * n * (n * columns[..., None] + ids) + n * which + ids
    hit = (held > 0)[..., None] & (place[..., None] == jnp.arange(2 * slots))
    return jnp.where(hit, value[..., None], 0).sum((-3, -2))


def spot(packed, blocks, in_product):
    at = packed - 1
    at = at >> blocks.bit_length() if in_product else at & (2 * blocks - 1)
    block = jnp.where(packed > 0, at >> (blocks.bit_length() - 1), 0)
    lane = jnp.where(packed > 0, at & (blocks - 1), blocks)
    return block, pl.ds(pl.multiple_of(lane * TILE, TILE), TILE)


def pick_kernel(info_ref, from_ref, out_ref, *, slots, blocks):
    for t in range(slots):
        at = jnp.maximum(info_ref[t] - 1, 0) & (2 * blocks - 1)
        rows = pl.ds(pl.multiple_of(at * LANES, LANES), LANES)
        out_ref[t * LANES : (t + 1) * LANES, :] = jnp.where(info_ref[t] > 0, from_ref[rows, :], 0.0)


def place_kernel(info_ref, own_ref, other_ref, out_ref, *, slots, blocks):
    out_ref[...] = jnp.zeros_like(out_ref)
    for base, ref in ((0, own_ref), (slots, other_ref)):
        for t in range(slots):
            block, lanes = spot(info_ref[base + t], blocks, False)

            @pl.when(info_ref[base + t] > 0)
            def _(block=block, lanes=lanes, ref=ref, t=t):
                rows = pl.ds(pl.multiple_of(block * LANES, LANES), LANES)
                out_ref[rows, lanes] = ref[t * LANES : (t + 1) * LANES, :]


def step_kernel(info_ref, own_ref, other_ref, out_ref, x_ref, hi_ref, lo_ref, left_ref, prod_ref,
                *, slots_in, slots_out, blocks):
    share, square = info_ref[0], info_ref[3]
    sharers = TILE // LANES
    whole = slice(0, blocks * TILE)
    x_ref[:, whole] = jnp.zeros((x_ref.shape[0], blocks * TILE), jnp.float32)
    prod_ref[:, blocks * TILE :] = jnp.zeros((blocks * LANES, TILE), jnp.float32)
    for base, ref in ((4, own_ref), (4 + slots_in, other_ref)):
        for t in range(slots_in):
            block, lanes = spot(info_ref[base + t], blocks, False)
            for s in range(sharers):
                at = pl.multiple_of(block * TILE + s * LANES, LANES)
                x_ref[pl.ds(at, LANES), lanes] = ref[s, t * LANES : (t + 1) * LANES, :]

    group = lax.broadcasted_iota(jnp.int32, (x_ref.shape[0], TILE), 1) // LANES
    for j in range(blocks):
        lanes = slice(j * TILE, (j + 1) * TILE)
        x = x_ref[:, lanes]
        hi = x.astype(jnp.bfloat16)
        hi_ref[:, lanes] = hi
        lo_ref[:, lanes] = (x - hi.astype(jnp.float32)).astype(jnp.bfloat16)
        half = slice(j // sharers * TILE, (j // sharers + 1) * TILE)
        turned = pltpu.roll(x, ((j - share) & (sharers - 1)) * LANES, 1)
        left_ref[:, half] = jnp.where(group == j % sharers, turned, left_ref[:, half])
    sign = jnp.where(square == 1, 1.0, -1.0)
    weight = jnp.where(square == 1, 0.0, 2.0)
    left = left_ref[...].T * sign
    a_hi = left.astype(jnp.bfloat16)
    a_lo = (left - a_hi.astype(jnp.float32)).astype(jnp.bfloat16)
    wide = 4 * TILE
    for j in range(blocks * TILE // wide):
        lanes = slice(j * wide, (j + 1) * wide)
        b_hi, b_lo = hi_ref[:, lanes], lo_ref[:, lanes]
        prod_ref[:, lanes] = (
            jnp.dot(a_hi, b_hi, preferred_element_type=jnp.float32)
            + jnp.dot(a_hi, b_lo, preferred_element_type=jnp.float32)
            + jnp.dot(a_lo, b_hi, preferred_element_type=jnp.float32)
        )

    for half in range(2):
        rows = pl.ds(pl.multiple_of(info_ref[1 + half] * LANES, LANES), LANES)
        mine = pl.ds(pl.multiple_of(half * TILE + share * LANES, LANES), LANES)
        prod_ref[rows, whole] = prod_ref[rows, whole] + weight * x_ref[mine, whole]

    first = 4 + 2 * slots_in

    def pick(t, _):
        block, lanes = spot(info_ref[first + t], blocks, True)
        rows = pl.ds(pl.multiple_of(block * LANES, LANES), LANES)
        out_ref[pl.ds(pl.multiple_of(t * LANES, LANES), LANES), :] = prod_ref[rows, lanes]
        return 0

    lax.fori_loop(0, out_ref.shape[0] // LANES, pick, 0, unroll=16)


def on_core(kernel, shape, scratch=()):
    vmem_spec, smem_spec = pl.BlockSpec(memory_space=pltpu.VMEM), pl.BlockSpec(memory_space=pltpu.SMEM)

    def call(info, *arrays):
        return pl.pallas_call(
            kernel,
            out_shape=jax.ShapeDtypeStruct(shape, jnp.float32),
            in_specs=[smem_spec] + [vmem_spec] * len(arrays),
            out_specs=vmem_spec,
            scratch_shapes=list(scratch),
            compiler_params=pltpu.CompilerParams(vmem_limit_bytes=48 * 1024 * 1024),
        )(info, *arrays)

    return call


def plane_groups():
    rows, layers = lax.axis_size("row"), lax.axis_size("depth")
    return [[(x * 2 + c) * layers + y for x in range(rows // 2) for y in range(layers)] for c in range(2)]


def in_plane(part):
    own = gather(part, ("row", "depth"), TILE // LANES, plane_groups())
    return own, swap_cores(own)


def sparse(own, other, natural, balanced, order, branch):
    rows, cols, layers = lax.axis_size("row"), lax.axis_size("col"), lax.axis_size("depth")
    row, col, layer = lax.axis_index("row"), lax.axis_index("col"), lax.axis_index("depth")
    core, share = row % 2, (row // 2) * layers + layer
    blocks = order.shape[0]
    whole = blocks * TILE
    layouts = [(natural, NATURAL, jnp.arange(blocks))] + [(balanced, BALANCED, order)] * (STEPS - 1)
    layouts = layouts + [layouts[0]]

    def of_plane(packed):
        packed = packed.reshape(cols, 2, -1)
        both = lax.dynamic_index_in_dim(packed, col, 0, keepdims=False)
        return jnp.where(core == 0, both, both[::-1]).reshape(-1)

    def for_planes(packed):
        packed = packed.reshape(cols // 4, 4, 2, -1)
        packed = lax.dynamic_index_in_dim(packed, core, 2, keepdims=False)
        twice = jnp.concatenate([packed, packed], axis=1)
        return lax.dynamic_slice_in_dim(twice, col % 4, 4, 1).transpose(1, 0, 2).reshape(-1)

    part = None
    for step in range(STEPS):
        now, slots_in, columns = layouts[step]
        then, slots_out, _ = layouts[step + 1]
        if step > 0:
            own, other = in_plane(part)
        info = jnp.concatenate(
            [
                share[None],
                lax.dynamic_slice_in_dim(columns, 2 * col, 2, 0),
                branch[step][None],
                of_plane(now),
                for_planes(then),
            ]
        ).astype(jnp.int32)
        wide = 2 * TILE
        out = on_core(
            functools.partial(step_kernel, slots_in=slots_in, slots_out=slots_out, blocks=blocks),
            (cols * slots_out * LANES, TILE),
            scratch=(
                pltpu.VMEM((wide, whole + TILE), jnp.float32),
                pltpu.VMEM((wide, whole), jnp.bfloat16),
                pltpu.VMEM((wide, whole), jnp.bfloat16),
                pltpu.VMEM((wide, blocks * LANES), jnp.float32),
                pltpu.VMEM((blocks * LANES, whole + TILE), jnp.float32),
            ),
        )(info, own, other)
        part = sum_along_col(out.reshape(4, cols // 4, slots_out * LANES, TILE))

    strips = on_core(
        functools.partial(place_kernel, slots=NATURAL, blocks=blocks), (2 * LANES, whole)
    )(of_plane(natural), part, swap_cores(part))
    sharers, height = TILE // LANES, whole // rows
    cut = strips.reshape(2 * LANES, rows // 2, 2, height)
    cut = lax.dynamic_index_in_dim(cut, core, 2, keepdims=False).transpose(1, 0, 2)
    cut = jnp.broadcast_to(cut[:, None], (rows // 2, layers) + cut.shape[1:]).reshape(sharers, 2 * LANES, height)
    back = exchange(cut, ("row", "depth"), plane_groups())
    back = back.reshape(sharers, 2, LANES, height).transpose(1, 0, 2, 3).reshape(2 * TILE, height)
    return back


def local(density, pattern, branch):
    rows, cols, layers = lax.axis_size("row"), lax.axis_size("col"), lax.axis_size("depth")
    row, col, layer = lax.axis_index("row"), lax.axis_index("col"), lax.axis_index("depth")
    height, width = density.shape
    blocks = rows * pattern.shape[0]
    tall = pattern.shape[0]
    cut = density.T.reshape(2, rows // 2, layers, LANES, tall, TILE)
    cut = lax.dynamic_index_in_dim(cut, layer, 2, keepdims=False).transpose(1, 0, 3, 2, 4)
    cut = cut.reshape(rows // 2, 2 * tall * LANES, TILE)
    marks = jnp.zeros((LANES, TILE), jnp.float32).at[:2, :tall].set(pattern.T.astype(jnp.float32))
    cut = jnp.concatenate([cut, jnp.broadcast_to(marks[None], (rows // 2,) + marks.shape)], axis=1)
    cut = jnp.broadcast_to(cut[:, None], (rows // 2, 2) + cut.shape[1:]).reshape((rows,) + cut.shape[1:])
    got = exchange(cut, "row")
    strips = got[:, : 2 * tall * LANES].reshape(rows, 2, tall * LANES, TILE)
    strips = strips.transpose(1, 0, 2, 3).reshape(2 * blocks * LANES, TILE)
    marks = got[:, 2 * tall * LANES : 2 * tall * LANES + 2, :tall].transpose(1, 0, 2).reshape(2, blocks)

    ids = jnp.arange(blocks)
    sent = jnp.zeros((LANES, TILE), jnp.float32).at[:2, :blocks].set(marks)
    steps = [(r, z, y, (z - r // 2 * layers - y) % cols) for r in range(rows) for z in range(cols) for y in range(layers)]
    ahead = lax.ppermute(
        sent,
        ("row", "col", "depth"),
        [((r * cols + z) * layers + y, (r * cols + to) * layers + y) for r, z, y, to in steps],
    )
    columns = 2 * col + jnp.arange(2)
    held = jnp.where(columns[:, None] == ids, 1, marks.astype(jnp.int32))
    mine = slot_list(held, columns, NATURAL).reshape(2, NATURAL)
    part = on_core(functools.partial(pick_kernel, slots=NATURAL, blocks=blocks), (NATURAL * LANES, TILE))(
        lax.dynamic_index_in_dim(mine, row % 2, 0, keepdims=False), strips
    )
    own, other = in_plane(jnp.concatenate([part, ahead]))
    seen = own[:, NATURAL * LANES : NATURAL * LANES + 2, :blocks].reshape(2 * cols, blocks)
    seen = lax.dynamic_slice_in_dim(jnp.concatenate([seen, seen]), 2 * (cols - col), 2 * cols, 0)
    keep = jnp.where(ids[:, None] == ids[None, :], 1, seen.astype(jnp.int32))
    order = column_order(keep)
    moved = jnp.dot((order[:, None] == ids).astype(jnp.float32), keep.astype(jnp.float32)).astype(jnp.int32)

    def in_pairs(rows_of):
        return rows_of.reshape((cols, 2) + rows_of.shape[1:])

    natural = slot_list(in_pairs(keep), in_pairs(ids), NATURAL)
    balanced = slot_list(in_pairs(moved), in_pairs(order), BALANCED)
    spare = jnp.stack(
        [2 * NATURAL - in_pairs(keep).sum((1, 2)), 2 * BALANCED - in_pairs(moved).sum((1, 2))]
    )
    purified = sparse(own, other, natural, balanced, order, branch)
    return lax.cond(spare.min() >= 0, lambda: purified.T, lambda: dense(density, pattern, branch))


def solution(mesh):
    in_specs = (P("row", "col"), P("row", "col"), P())
    out_specs = P("row", "col")
    return jax.shard_map(local, mesh=mesh, in_specs=in_specs, out_specs=out_specs, check_vma=False)
```

```python
import functools

import jax
import jax.numpy as jnp
from jax import lax
from jax.experimental import pallas as pl
from jax.experimental.pallas import tpu as pltpu
from jax.sharding import PartitionSpec as P

TILE = 128
STEPS = 4
LANES = 8
NATURAL = 18
BALANCED = 14


def exchange(parts, axis, groups=None):
    return lax.all_to_all(parts, axis, 0, 0, axis_index_groups=groups, tiled=True)


def gather(part, axis, members, groups=None):
    return exchange(jnp.broadcast_to(part[None], (members,) + part.shape), axis, groups)


def shifted(parts, by):
    cols = lax.axis_size("col")
    return lax.ppermute(parts, "col", [(z, (z + by) % cols) for z in range(cols)])


def sum_along_col(ahead):
    cols = lax.axis_size("col")
    far = [[c + 4 * m for m in range(cols // 4)] for c in range(4)]
    near = ahead[0] + shifted(ahead[1], 1) + shifted(ahead[3], -1)
    near = near + jnp.concatenate([shifted(ahead[2][:2], 2), shifted(ahead[2][2:], -2)])
    return exchange(near, "col", far).sum(0)


def sum_slots(own, one, two):
    rows, cols, core = lax.axis_size("row"), lax.axis_size("col"), lax.axis_index("row") % 2
    far = [[c + 4 * m for m in range(cols // 4)] for c in range(4)]

    def apart(value, by):
        steps = [(r, z, (z + by * (1 - 2 * (r % 2))) % cols) for r in range(rows) for z in range(cols)]
        return lax.ppermute(value, ("row", "col"), [(r * cols + z, r * cols + to) for r, z, to in steps])

    one, two = apart(one, 1), apart(two, 2)
    half = lax.broadcasted_iota(jnp.int32, (one.shape[0], 1, 1, 1), 0) // two.shape[0]
    got = one + jnp.where(half == core, jnp.concatenate([two, two]), 0.0)
    theirs = swap_cores(lax.dynamic_index_in_dim(got, 1 - core, 1, keepdims=False))
    near = own + lax.dynamic_index_in_dim(got, core, 1, keepdims=False) + theirs
    return exchange(near, "col", far).sum(0)


def swap_cores(value):
    return lax.ppermute(value, "row", [(i, i ^ 1) for i in range(lax.axis_size("row"))])


def dense(density, pattern, branch):
    rows, cols = lax.axis_size("row"), lax.axis_size("col")
    layers = lax.axis_size("depth")
    row, col, layer = lax.axis_index("row"), lax.axis_index("col"), lax.axis_index("depth")
    height, width = density.shape
    sub = width // layers
    core = row % 2
    cores_apart = [[x * 2 + c for x in range(rows // 2)] for c in range(2)]

    row_ids = lax.broadcasted_iota(jnp.int32, pattern.shape, 0) + row * pattern.shape[0]
    col_ids = lax.broadcasted_iota(jnp.int32, pattern.shape, 1) + col * pattern.shape[1]
    tiles = jnp.where(row_ids == col_ids, 1, pattern).T.astype(jnp.float32)
    keep = jnp.repeat(jnp.repeat(tiles, TILE, axis=0), TILE, axis=1)
    keep_part = lax.dynamic_slice_in_dim(keep, layer * sub, sub, 0)

    panel = density.T * keep
    part = lax.dynamic_slice_in_dim(panel, layer * sub, sub, 0)
    for step in range(STEPS):
        mine = panel.T.reshape(height // width, layers, sub, width)
        mine = lax.dynamic_index_in_dim(mine, layer, 1, keepdims=False)
        own = gather(mine, "row", rows // 2, cores_apart)
        other = swap_cores(own)

        def product(left, panel=panel):
            out = jnp.dot(
                left.reshape(-1, width), panel, precision=lax.Precision.HIGH, preferred_element_type=jnp.float32
            )
            return out.reshape(rows // 2, 2, sub, height)

        both = jnp.stack([product(own), product(other)])

        def of_class(k, both=both):
            k = k % 4
            start = ((k // 2) ^ core, 0, k % 2, 0, 0)
            out = lax.dynamic_slice(both, start, (1, rows // 2, 1, sub, height))
            return out.reshape(rows // 2, sub, height)

        squared = sum_along_col([of_class(col + q) for q in range(4)])
        part = keep_part * jnp.where(branch[step] == 1, squared, 2.0 * part - squared)
        panel = gather(part, "depth", layers).reshape(width, height)
    return panel.T


def column_order(keep):
    n = keep.shape[0]
    load = keep.sum(0)
    ids = jnp.arange(n)
    ahead = (load[None, :] > load[:, None]) | ((load[None, :] == load[:, None]) & (ids[None, :] < ids[:, None]))
    rank = ahead.astype(jnp.int32).sum(1)
    place = jnp.where(rank < n // 2, 2 * rank, 2 * (n - 1 - rank) + 1)
    return jnp.where(place[None, :] == ids[:, None], ids[None, :], 0).sum(1)


def slot_list(held, columns, slots):
    n = held.shape[-1]
    ids = jnp.arange(n)
    upto = (ids[:, None] <= ids[None, :]).astype(jnp.float32)
    count = jnp.dot(held.astype(jnp.float32), upto).astype(jnp.int32)
    which = jnp.arange(2)[:, None]
    place = count - 1 + which * count[..., :1, -1:]
    value = 1 + 2 * n * (n * columns[..., None] + ids) + n * which + ids
    hit = (held > 0)[..., None] & (place[..., None] == jnp.arange(2 * slots))
    return jnp.where(hit, value[..., None], 0).sum((-3, -2))


def spot(packed, blocks, in_product):
    at = packed - 1
    at = at >> blocks.bit_length() if in_product else at & (2 * blocks - 1)
    block = jnp.where(packed > 0, at >> (blocks.bit_length() - 1), 0)
    lane = jnp.where(packed > 0, at & (blocks - 1), blocks)
    return block, pl.ds(pl.multiple_of(lane * TILE, TILE), TILE)


def pick_kernel(info_ref, from_ref, out_ref, *, slots, blocks):
    for t in range(slots):
        at = jnp.maximum(info_ref[t] - 1, 0) & (2 * blocks - 1)
        rows = pl.ds(pl.multiple_of(at * LANES, LANES), LANES)
        out_ref[t * LANES : (t + 1) * LANES, :] = jnp.where(info_ref[t] > 0, from_ref[rows, :], 0.0)


def place_kernel(info_ref, own_ref, other_ref, out_ref, *, slots, blocks):
    out_ref[...] = jnp.zeros_like(out_ref)
    for base, ref in ((0, own_ref), (slots, other_ref)):
        for t in range(slots):
            block, lanes = spot(info_ref[base + t], blocks, False)

            @pl.when(info_ref[base + t] > 0)
            def _(block=block, lanes=lanes, ref=ref, t=t):
                rows = pl.ds(pl.multiple_of(block * LANES, LANES), LANES)
                out_ref[rows, lanes] = ref[t * LANES : (t + 1) * LANES, :]


def step_kernel(info_ref, own_ref, other_ref, out_ref, x_ref, hi_ref, lo_ref, left_ref, prod_ref,
                *, slots_in, slots_out, blocks):
    share, square = info_ref[0], info_ref[3]
    sharers = TILE // LANES
    whole = slice(0, blocks * TILE)
    x_ref[:, whole] = jnp.zeros((x_ref.shape[0], blocks * TILE), jnp.float32)
    prod_ref[:, blocks * TILE :] = jnp.zeros((blocks * LANES, TILE), jnp.float32)
    for base, ref in ((4, own_ref), (4 + slots_in, other_ref)):
        for t in range(slots_in):
            block, lanes = spot(info_ref[base + t], blocks, False)
            for s in range(sharers):
                at = pl.multiple_of(block * TILE + s * LANES, LANES)
                x_ref[pl.ds(at, LANES), lanes] = ref[s, t * LANES : (t + 1) * LANES, :]

    group = lax.broadcasted_iota(jnp.int32, (x_ref.shape[0], TILE), 1) // LANES
    for j in range(blocks):
        lanes = slice(j * TILE, (j + 1) * TILE)
        x = x_ref[:, lanes]
        hi = x.astype(jnp.bfloat16)
        hi_ref[:, lanes] = hi
        lo_ref[:, lanes] = (x - hi.astype(jnp.float32)).astype(jnp.bfloat16)
        half = slice(j // sharers * TILE, (j // sharers + 1) * TILE)
        turned = pltpu.roll(x, ((j - share) & (sharers - 1)) * LANES, 1)
        left_ref[:, half] = jnp.where(group == j % sharers, turned, left_ref[:, half])
    sign = jnp.where(square == 1, 1.0, -1.0)
    weight = jnp.where(square == 1, 0.0, 2.0)
    left = left_ref[...].T * sign
    a_hi = left.astype(jnp.bfloat16)
    a_lo = (left - a_hi.astype(jnp.float32)).astype(jnp.bfloat16)
    wide = 4 * TILE
    for j in range(blocks * TILE // wide):
        lanes = slice(j * wide, (j + 1) * wide)
        b_hi, b_lo = hi_ref[:, lanes], lo_ref[:, lanes]
        prod_ref[:, lanes] = (
            jnp.dot(a_hi, b_hi, preferred_element_type=jnp.float32)
            + jnp.dot(a_hi, b_lo, preferred_element_type=jnp.float32)
            + jnp.dot(a_lo, b_hi, preferred_element_type=jnp.float32)
        )

    for half in range(2):
        rows = pl.ds(pl.multiple_of(info_ref[1 + half] * LANES, LANES), LANES)
        mine = pl.ds(pl.multiple_of(half * TILE + share * LANES, LANES), LANES)
        prod_ref[rows, whole] = prod_ref[rows, whole] + weight * x_ref[mine, whole]

    first = 4 + 2 * slots_in

    def pick(t, _):
        block, lanes = spot(info_ref[first + t], blocks, True)
        rows = pl.ds(pl.multiple_of(block * LANES, LANES), LANES)
        out_ref[pl.ds(pl.multiple_of(t * LANES, LANES), LANES), :] = prod_ref[rows, lanes]
        return 0

    lax.fori_loop(0, out_ref.shape[0] // LANES, pick, 0, unroll=16)


def on_core(kernel, shape, scratch=()):
    vmem_spec, smem_spec = pl.BlockSpec(memory_space=pltpu.VMEM), pl.BlockSpec(memory_space=pltpu.SMEM)

    def call(info, *arrays):
        return pl.pallas_call(
            kernel,
            out_shape=jax.ShapeDtypeStruct(shape, jnp.float32),
            in_specs=[smem_spec] + [vmem_spec] * len(arrays),
            out_specs=vmem_spec,
            scratch_shapes=list(scratch),
            compiler_params=pltpu.CompilerParams(vmem_limit_bytes=48 * 1024 * 1024),
        )(info, *arrays)

    return call


def plane_groups():
    rows, layers = lax.axis_size("row"), lax.axis_size("depth")
    return [[(x * 2 + c) * layers + y for x in range(rows // 2) for y in range(layers)] for c in range(2)]


def in_plane(part):
    own = gather(part, ("row", "depth"), TILE // LANES, plane_groups())
    return own, swap_cores(own)


def sparse(own, other, natural, balanced, order, branch):
    rows, cols, layers = lax.axis_size("row"), lax.axis_size("col"), lax.axis_size("depth")
    row, col, layer = lax.axis_index("row"), lax.axis_index("col"), lax.axis_index("depth")
    core, share = row % 2, (row // 2) * layers + layer
    blocks = order.shape[0]
    whole = blocks * TILE
    layouts = [(natural, NATURAL, jnp.arange(blocks))] + [(balanced, BALANCED, order)] * (STEPS - 1)
    layouts = layouts + [layouts[0]]

    def of_plane(packed):
        packed = packed.reshape(cols, 2, -1)
        both = lax.dynamic_index_in_dim(packed, col, 0, keepdims=False)
        return jnp.where(core == 0, both, both[::-1]).reshape(-1)

    def for_planes(packed):
        packed = packed.reshape(cols // 4, 4, -1)
        slots = packed.shape[2] // 2

        def of_class(by):
            return lax.dynamic_index_in_dim(packed, (col + by) % 4, 1, keepdims=False)

        own = lax.dynamic_slice_in_dim(of_class(0), core * slots, slots, 1)
        two = lax.dynamic_slice_in_dim(of_class(2), core * (cols // 8), cols // 8, 0)
        return jnp.concatenate([v.reshape(-1) for v in (own, of_class(1 + 2 * core), two)])

    part = None
    for step in range(STEPS):
        now, slots_in, columns = layouts[step]
        then, slots_out, _ = layouts[step + 1]
        if step > 0:
            own, other = in_plane(part)
        info = jnp.concatenate(
            [
                share[None],
                lax.dynamic_slice_in_dim(columns, 2 * col, 2, 0),
                branch[step][None],
                of_plane(now),
                for_planes(then),
            ]
        ).astype(jnp.int32)
        wide = 2 * TILE
        out = on_core(
            functools.partial(step_kernel, slots_in=slots_in, slots_out=slots_out, blocks=blocks),
            (cols * slots_out * LANES, TILE),
            scratch=(
                pltpu.VMEM((wide, whole + TILE), jnp.float32),
                pltpu.VMEM((wide, whole), jnp.bfloat16),
                pltpu.VMEM((wide, whole), jnp.bfloat16),
                pltpu.VMEM((wide, blocks * LANES), jnp.float32),
                pltpu.VMEM((blocks * LANES, whole + TILE), jnp.float32),
            ),
        )(info, own, other)
        quads, tall = cols // 4, slots_out * LANES
        own, one, two = jnp.split(out, [quads * tall, 3 * quads * tall])
        part = sum_slots(
            own.reshape(quads, tall, TILE), one.reshape(quads, 2, tall, TILE), two.reshape(-1, 2, tall, TILE)
        )

    strips = on_core(
        functools.partial(place_kernel, slots=NATURAL, blocks=blocks), (2 * LANES, whole)
    )(of_plane(natural), part, swap_cores(part))
    sharers, height = TILE // LANES, whole // rows
    cut = strips.reshape(2 * LANES, rows // 2, 2, height)
    cut = lax.dynamic_index_in_dim(cut, core, 2, keepdims=False).transpose(1, 0, 2)
    cut = jnp.broadcast_to(cut[:, None], (rows // 2, layers) + cut.shape[1:]).reshape(sharers, 2 * LANES, height)
    back = exchange(cut, ("row", "depth"), plane_groups())
    back = back.reshape(sharers, 2, LANES, height).transpose(1, 0, 2, 3).reshape(2 * TILE, height)
    return back


def local(density, pattern, branch):
    rows, cols, layers = lax.axis_size("row"), lax.axis_size("col"), lax.axis_size("depth")
    row, col, layer = lax.axis_index("row"), lax.axis_index("col"), lax.axis_index("depth")
    height, width = density.shape
    blocks = rows * pattern.shape[0]
    tall = pattern.shape[0]
    cut = density.T.reshape(2, rows // 2, layers, LANES, tall, TILE)
    cut = lax.dynamic_index_in_dim(cut, layer, 2, keepdims=False).transpose(1, 0, 3, 2, 4)
    cut = cut.reshape(rows // 2, 2 * tall * LANES, TILE)
    marks = jnp.zeros((LANES, TILE), jnp.float32).at[:2, :tall].set(pattern.T.astype(jnp.float32))
    cut = jnp.concatenate([cut, jnp.broadcast_to(marks[None], (rows // 2,) + marks.shape)], axis=1)
    cut = jnp.broadcast_to(cut[:, None], (rows // 2, 2) + cut.shape[1:]).reshape((rows,) + cut.shape[1:])
    got = exchange(cut, "row")
    strips = got[:, : 2 * tall * LANES].reshape(rows, 2, tall * LANES, TILE)
    strips = strips.transpose(1, 0, 2, 3).reshape(2 * blocks * LANES, TILE)
    marks = got[:, 2 * tall * LANES : 2 * tall * LANES + 2, :tall].transpose(1, 0, 2).reshape(2, blocks)

    ids = jnp.arange(blocks)
    sent = jnp.zeros((LANES, TILE), jnp.float32).at[:2, :blocks].set(marks)
    steps = [(r, z, y, (z - r // 2 * layers - y) % cols) for r in range(rows) for z in range(cols) for y in range(layers)]
    ahead = lax.ppermute(
        sent,
        ("row", "col", "depth"),
        [((r * cols + z) * layers + y, (r * cols + to) * layers + y) for r, z, y, to in steps],
    )
    columns = 2 * col + jnp.arange(2)
    held = jnp.where(columns[:, None] == ids, 1, marks.astype(jnp.int32))
    mine = slot_list(held, columns, NATURAL).reshape(2, NATURAL)
    part = on_core(functools.partial(pick_kernel, slots=NATURAL, blocks=blocks), (NATURAL * LANES, TILE))(
        lax.dynamic_index_in_dim(mine, row % 2, 0, keepdims=False), strips
    )
    own, other = in_plane(jnp.concatenate([part, ahead]))
    seen = own[:, NATURAL * LANES : NATURAL * LANES + 2, :blocks].reshape(2 * cols, blocks)
    seen = lax.dynamic_slice_in_dim(jnp.concatenate([seen, seen]), 2 * (cols - col), 2 * cols, 0)
    keep = jnp.where(ids[:, None] == ids[None, :], 1, seen.astype(jnp.int32))
    order = column_order(keep)
    moved = jnp.dot((order[:, None] == ids).astype(jnp.float32), keep.astype(jnp.float32)).astype(jnp.int32)

    def in_pairs(rows_of):
        return rows_of.reshape((cols, 2) + rows_of.shape[1:])

    natural = slot_list(in_pairs(keep), in_pairs(ids), NATURAL)
    balanced = slot_list(in_pairs(moved), in_pairs(order), BALANCED)
    spare = jnp.stack(
        [2 * NATURAL - in_pairs(keep).sum((1, 2)), 2 * BALANCED - in_pairs(moved).sum((1, 2))]
    )
    purified = sparse(own, other, natural, balanced, order, branch)
    return lax.cond(spare.min() >= 0, lambda: purified.T, lambda: dense(density, pattern, branch))


def solution(mesh):
    in_specs = (P("row", "col"), P("row", "col"), P())
    out_specs = P("row", "col")
    return jax.shard_map(local, mesh=mesh, in_specs=in_specs, out_specs=out_specs, check_vma=False)
```

```python
import functools

import jax
import jax.numpy as jnp
from jax import lax
from jax.experimental import pallas as pl
from jax.experimental.pallas import tpu as pltpu
from jax.sharding import PartitionSpec as P

TILE = 128
STEPS = 4
LANES = 8
NATURAL = 18
BALANCED = 14


def exchange(parts, axis, groups=None):
    return lax.all_to_all(parts, axis, 0, 0, axis_index_groups=groups, tiled=True)


def gather(part, axis, members, groups=None):
    return exchange(jnp.broadcast_to(part[None], (members,) + part.shape), axis, groups)


def shifted(parts, by):
    cols = lax.axis_size("col")
    return lax.ppermute(parts, "col", [(z, (z + by) % cols) for z in range(cols)])


def sum_along_col(ahead):
    cols = lax.axis_size("col")
    far = [[c + 4 * m for m in range(cols // 4)] for c in range(4)]
    near = ahead[0] + shifted(ahead[1], 1) + shifted(ahead[3], -1)
    near = near + jnp.concatenate([shifted(ahead[2][:2], 2), shifted(ahead[2][2:], -2)])
    return exchange(near, "col", far).sum(0)


def swap_cores(value):
    return lax.ppermute(value, "row", [(i, i ^ 1) for i in range(lax.axis_size("row"))])


def dense(density, pattern, branch):
    rows, cols = lax.axis_size("row"), lax.axis_size("col")
    layers = lax.axis_size("depth")
    row, col, layer = lax.axis_index("row"), lax.axis_index("col"), lax.axis_index("depth")
    height, width = density.shape
    sub = width // layers
    core = row % 2
    cores_apart = [[x * 2 + c for x in range(rows // 2)] for c in range(2)]

    row_ids = lax.broadcasted_iota(jnp.int32, pattern.shape, 0) + row * pattern.shape[0]
    col_ids = lax.broadcasted_iota(jnp.int32, pattern.shape, 1) + col * pattern.shape[1]
    tiles = jnp.where(row_ids == col_ids, 1, pattern).T.astype(jnp.float32)
    keep = jnp.repeat(jnp.repeat(tiles, TILE, axis=0), TILE, axis=1)
    keep_part = lax.dynamic_slice_in_dim(keep, layer * sub, sub, 0)

    panel = density.T * keep
    part = lax.dynamic_slice_in_dim(panel, layer * sub, sub, 0)
    for step in range(STEPS):
        mine = panel.T.reshape(height // width, layers, sub, width)
        mine = lax.dynamic_index_in_dim(mine, layer, 1, keepdims=False)
        own = gather(mine, "row", rows // 2, cores_apart)
        other = swap_cores(own)

        def product(left, panel=panel):
            out = jnp.dot(
                left.reshape(-1, width), panel, precision=lax.Precision.HIGH, preferred_element_type=jnp.float32
            )
            return out.reshape(rows // 2, 2, sub, height)

        both = jnp.stack([product(own), product(other)])

        def of_class(k, both=both):
            k = k % 4
            start = ((k // 2) ^ core, 0, k % 2, 0, 0)
            out = lax.dynamic_slice(both, start, (1, rows // 2, 1, sub, height))
            return out.reshape(rows // 2, sub, height)

        squared = sum_along_col([of_class(col + q) for q in range(4)])
        part = keep_part * jnp.where(branch[step] == 1, squared, 2.0 * part - squared)
        panel = gather(part, "depth", layers).reshape(width, height)
    return panel.T


def column_order(keep):
    n = keep.shape[0]
    load = keep.sum(0)
    ids = jnp.arange(n)
    ahead = (load[None, :] > load[:, None]) | ((load[None, :] == load[:, None]) & (ids[None, :] < ids[:, None]))
    rank = ahead.astype(jnp.int32).sum(1)
    place = jnp.where(rank < n // 2, 2 * rank, 2 * (n - 1 - rank) + 1)
    return jnp.where(place[None, :] == ids[:, None], ids[None, :], 0).sum(1)


def slot_list(held, columns, slots):
    n = held.shape[-1]
    ids = jnp.arange(n)
    upto = (ids[:, None] <= ids[None, :]).astype(jnp.float32)
    count = jnp.dot(held.astype(jnp.float32), upto).astype(jnp.int32)
    which = jnp.arange(2)[:, None]
    place = count - 1 + which * count[..., :1, -1:]
    value = 1 + 2 * n * (n * columns[..., None] + ids) + n * which + ids
    hit = (held > 0)[..., None] & (place[..., None] == jnp.arange(2 * slots))
    return jnp.where(hit, value[..., None], 0).sum((-3, -2))


def spot(packed, blocks, in_product):
    at = packed - 1
    at = at >> blocks.bit_length() if in_product else at & (2 * blocks - 1)
    block = jnp.where(packed > 0, at >> (blocks.bit_length() - 1), 0)
    lane = jnp.where(packed > 0, at & (blocks - 1), blocks)
    return block, pl.ds(pl.multiple_of(lane * TILE, TILE), TILE)


def pick_kernel(info_ref, from_ref, out_ref, *, slots, blocks):
    for t in range(slots):
        at = jnp.maximum(info_ref[t] - 1, 0) & (2 * blocks - 1)
        rows = pl.ds(pl.multiple_of(at // blocks * LANES, LANES), LANES)
        lanes = pl.ds(pl.multiple_of(at % blocks * TILE, TILE), TILE)
        out_ref[t * LANES : (t + 1) * LANES, :] = jnp.where(info_ref[t] > 0, from_ref[rows, lanes], 0.0)


def place_kernel(info_ref, own_ref, other_ref, out_ref, *, slots, blocks):
    out_ref[...] = jnp.zeros_like(out_ref)
    for base, ref in ((0, own_ref), (slots, other_ref)):
        for t in range(slots):
            block, lanes = spot(info_ref[base + t], blocks, False)

            @pl.when(info_ref[base + t] > 0)
            def _(block=block, lanes=lanes, ref=ref, t=t):
                rows = pl.ds(pl.multiple_of(block * LANES, LANES), LANES)
                out_ref[rows, lanes] = ref[t * LANES : (t + 1) * LANES, :]


def step_kernel(info_ref, own_ref, other_ref, out_ref, x_ref, hi_ref, lo_ref, left_ref, prod_ref,
                *, slots_in, slots_out, blocks):
    share, square = info_ref[0], info_ref[3]
    sharers = TILE // LANES
    whole = slice(0, blocks * TILE)
    x_ref[:, whole] = jnp.zeros((x_ref.shape[0], blocks * TILE), jnp.float32)
    prod_ref[:, blocks * TILE :] = jnp.zeros((blocks * LANES, TILE), jnp.float32)
    for base, ref in ((4, own_ref), (4 + slots_in, other_ref)):
        for t in range(slots_in):
            block, lanes = spot(info_ref[base + t], blocks, False)
            for s in range(sharers):
                at = pl.multiple_of(block * TILE + s * LANES, LANES)
                x_ref[pl.ds(at, LANES), lanes] = ref[s, t * LANES : (t + 1) * LANES, :]

    group = lax.broadcasted_iota(jnp.int32, (x_ref.shape[0], TILE), 1) // LANES
    for j in range(blocks):
        lanes = slice(j * TILE, (j + 1) * TILE)
        x = x_ref[:, lanes]
        hi = x.astype(jnp.bfloat16)
        hi_ref[:, lanes] = hi
        lo_ref[:, lanes] = (x - hi.astype(jnp.float32)).astype(jnp.bfloat16)
        half = slice(j // sharers * TILE, (j // sharers + 1) * TILE)
        turned = pltpu.roll(x, ((j - share) & (sharers - 1)) * LANES, 1)
        left_ref[:, half] = jnp.where(group == j % sharers, turned, left_ref[:, half])
    sign = jnp.where(square == 1, 1.0, -1.0)
    weight = jnp.where(square == 1, 0.0, 2.0)
    left = left_ref[...].T * sign
    a_hi = left.astype(jnp.bfloat16)
    a_lo = (left - a_hi.astype(jnp.float32)).astype(jnp.bfloat16)
    wide = 4 * TILE
    for j in range(blocks * TILE // wide):
        lanes = slice(j * wide, (j + 1) * wide)
        b_hi, b_lo = hi_ref[:, lanes], lo_ref[:, lanes]
        prod_ref[:, lanes] = (
            jnp.dot(a_hi, b_hi, preferred_element_type=jnp.float32)
            + jnp.dot(a_hi, b_lo, preferred_element_type=jnp.float32)
            + jnp.dot(a_lo, b_hi, preferred_element_type=jnp.float32)
        )

    for half in range(2):
        rows = pl.ds(pl.multiple_of(info_ref[1 + half] * LANES, LANES), LANES)
        mine = pl.ds(pl.multiple_of(half * TILE + share * LANES, LANES), LANES)
        prod_ref[rows, whole] = prod_ref[rows, whole] + weight * x_ref[mine, whole]

    first = 4 + 2 * slots_in

    def pick(t, _):
        block, lanes = spot(info_ref[first + t], blocks, True)
        rows = pl.ds(pl.multiple_of(block * LANES, LANES), LANES)
        out_ref[pl.ds(pl.multiple_of(t * LANES, LANES), LANES), :] = prod_ref[rows, lanes]
        return 0

    lax.fori_loop(0, out_ref.shape[0] // LANES, pick, 0, unroll=16)


def on_core(kernel, shape, scratch=()):
    vmem_spec, smem_spec = pl.BlockSpec(memory_space=pltpu.VMEM), pl.BlockSpec(memory_space=pltpu.SMEM)

    def call(info, *arrays):
        return pl.pallas_call(
            kernel,
            out_shape=jax.ShapeDtypeStruct(shape, jnp.float32),
            in_specs=[smem_spec] + [vmem_spec] * len(arrays),
            out_specs=vmem_spec,
            scratch_shapes=list(scratch),
            compiler_params=pltpu.CompilerParams(vmem_limit_bytes=48 * 1024 * 1024),
        )(info, *arrays)

    return call


def plane_groups():
    rows, layers = lax.axis_size("row"), lax.axis_size("depth")
    return [[(x * 2 + c) * layers + y for x in range(rows // 2) for y in range(layers)] for c in range(2)]


def in_plane(part):
    own = gather(part, ("row", "depth"), TILE // LANES, plane_groups())
    return own, swap_cores(own)


def sparse(own, other, natural, balanced, order, branch):
    rows, cols, layers = lax.axis_size("row"), lax.axis_size("col"), lax.axis_size("depth")
    row, col, layer = lax.axis_index("row"), lax.axis_index("col"), lax.axis_index("depth")
    core, share = row % 2, (row // 2) * layers + layer
    blocks = order.shape[0]
    whole = blocks * TILE
    layouts = [(natural, NATURAL, jnp.arange(blocks))] + [(balanced, BALANCED, order)] * (STEPS - 1)
    layouts = layouts + [layouts[0]]

    def of_plane(packed):
        packed = packed.reshape(cols, 2, -1)
        both = lax.dynamic_index_in_dim(packed, col, 0, keepdims=False)
        return jnp.where(core == 0, both, both[::-1]).reshape(-1)

    def for_planes(packed):
        packed = packed.reshape(cols // 4, 4, 2, -1)
        packed = lax.dynamic_index_in_dim(packed, core, 2, keepdims=False)
        twice = jnp.concatenate([packed, packed], axis=1)
        return lax.dynamic_slice_in_dim(twice, col % 4, 4, 1).transpose(1, 0, 2).reshape(-1)

    part = None
    for step in range(STEPS):
        now, slots_in, columns = layouts[step]
        then, slots_out, _ = layouts[step + 1]
        if step > 0:
            own, other = in_plane(part)
        info = jnp.concatenate(
            [
                share[None],
                lax.dynamic_slice_in_dim(columns, 2 * col, 2, 0),
                branch[step][None],
                of_plane(now),
                for_planes(then),
            ]
        ).astype(jnp.int32)
        wide = 2 * TILE
        out = on_core(
            functools.partial(step_kernel, slots_in=slots_in, slots_out=slots_out, blocks=blocks),
            (cols * slots_out * LANES, TILE),
            scratch=(
                pltpu.VMEM((wide, whole + TILE), jnp.float32),
                pltpu.VMEM((wide, whole), jnp.bfloat16),
                pltpu.VMEM((wide, whole), jnp.bfloat16),
                pltpu.VMEM((wide, blocks * LANES), jnp.float32),
                pltpu.VMEM((blocks * LANES, whole + TILE), jnp.float32),
            ),
        )(info, own, other)
        part = sum_along_col(out.reshape(4, cols // 4, slots_out * LANES, TILE))

    strips = on_core(
        functools.partial(place_kernel, slots=NATURAL, blocks=blocks), (2 * LANES, whole)
    )(of_plane(natural), part, swap_cores(part))
    sharers, height = TILE // LANES, whole // rows
    cut = strips.reshape(2 * LANES, rows // 2, 2, height)
    cut = lax.dynamic_index_in_dim(cut, core, 2, keepdims=False).transpose(1, 0, 2)
    cut = jnp.broadcast_to(cut[:, None], (rows // 2, layers) + cut.shape[1:]).reshape(sharers, 2 * LANES, height)
    back = exchange(cut, ("row", "depth"), plane_groups())
    back = back.reshape(sharers, 2, LANES, height).transpose(1, 0, 2, 3).reshape(2 * TILE, height)
    return back.T


def local(density, pattern, branch):
    rows, cols, layers = lax.axis_size("row"), lax.axis_size("col"), lax.axis_size("depth")
    row, col, layer = lax.axis_index("row"), lax.axis_index("col"), lax.axis_index("depth")
    height, width = density.shape
    blocks = rows * pattern.shape[0]
    cut = density.T.reshape(2, rows // 2, layers, LANES, height)
    cut = lax.dynamic_index_in_dim(cut, layer, 2, keepdims=False).transpose(1, 0, 2, 3)
    cut = cut.reshape(rows // 2, 2 * LANES, height)
    marks = jnp.zeros((LANES, height), jnp.float32).at[:2, : pattern.shape[0]].set(pattern.T.astype(jnp.float32))
    cut = jnp.concatenate([cut, jnp.broadcast_to(marks[None], (rows // 2,) + marks.shape)], axis=1)
    cut = jnp.broadcast_to(cut[:, None], (rows // 2, 2) + cut.shape[1:]).reshape((rows,) + cut.shape[1:])
    got = exchange(cut, "row")
    strips = got[:, : 2 * LANES].transpose(1, 0, 2).reshape(2 * LANES, rows * height)
    marks = got[:, 2 * LANES : 2 * LANES + 2, : pattern.shape[0]].transpose(1, 0, 2).reshape(2, blocks)

    ids = jnp.arange(blocks)
    sent = jnp.zeros((LANES, TILE), jnp.float32).at[:2, :blocks].set(marks)
    steps = [(r, z, y, (z - r // 2 * layers - y) % cols) for r in range(rows) for z in range(cols) for y in range(layers)]
    ahead = lax.ppermute(
        sent,
        ("row", "col", "depth"),
        [((r * cols + z) * layers + y, (r * cols + to) * layers + y) for r, z, y, to in steps],
    )
    columns = 2 * col + jnp.arange(2)
    held = jnp.where(columns[:, None] == ids, 1, marks.astype(jnp.int32))
    mine = slot_list(held, columns, NATURAL).reshape(2, NATURAL)
    part = on_core(functools.partial(pick_kernel, slots=NATURAL, blocks=blocks), (NATURAL * LANES, TILE))(
        lax.dynamic_index_in_dim(mine, row % 2, 0, keepdims=False), strips
    )
    own, other = in_plane(jnp.concatenate([part, ahead]))
    seen = own[:, NATURAL * LANES : NATURAL * LANES + 2, :blocks].reshape(2 * cols, blocks)
    seen = lax.dynamic_slice_in_dim(jnp.concatenate([seen, seen]), 2 * (cols - col), 2 * cols, 0)
    keep = jnp.where(ids[:, None] == ids[None, :], 1, seen.astype(jnp.int32))
    order = column_order(keep)
    moved = jnp.dot((order[:, None] == ids).astype(jnp.float32), keep.astype(jnp.float32)).astype(jnp.int32)

    def in_pairs(rows_of):
        return rows_of.reshape((cols, 2) + rows_of.shape[1:])

    natural = slot_list(in_pairs(keep), in_pairs(ids), NATURAL)
    balanced = slot_list(in_pairs(moved), in_pairs(order), BALANCED)
    spare = jnp.stack(
        [2 * NATURAL - in_pairs(keep).sum((1, 2)), 2 * BALANCED - in_pairs(moved).sum((1, 2))]
    )
    purified = sparse(own, other, natural, balanced, order, branch)
    return lax.cond(spare.min() >= 0, lambda: purified, lambda: dense(density, pattern, branch))


def solution(mesh):
    in_specs = (P("row", "col"), P("row", "col"), P())
    out_specs = P("row", "col")
    return jax.shard_map(local, mesh=mesh, in_specs=in_specs, out_specs=out_specs, check_vma=False)
```

```python
import functools

import jax
import jax.numpy as jnp
from jax import lax
from jax.experimental import pallas as pl
from jax.experimental.pallas import tpu as pltpu
from jax.sharding import PartitionSpec as P

TILE = 128
STEPS = 4
LANES = 8
NATURAL = 18
BALANCED = 14


def exchange(parts, axis, groups=None):
    return lax.all_to_all(parts, axis, 0, 0, axis_index_groups=groups, tiled=True)


def gather(part, axis, members, groups=None):
    return exchange(jnp.broadcast_to(part[None], (members,) + part.shape), axis, groups)


def shifted(parts, by):
    cols = lax.axis_size("col")
    return lax.ppermute(parts, "col", [(z, (z + by) % cols) for z in range(cols)])


def sum_along_col(ahead):
    cols = lax.axis_size("col")
    far = [[c + 4 * m for m in range(cols // 4)] for c in range(4)]
    near = ahead[0] + shifted(ahead[1], 1) + shifted(ahead[3], -1)
    near = near + jnp.concatenate([shifted(ahead[2][:2], 2), shifted(ahead[2][2:], -2)])
    return exchange(near, "col", far).sum(0)


def sum_slots(pair, up, down):
    cols = lax.axis_size("col")
    far = [[c + 4 * m for m in range(cols // 4)] for c in range(4)]
    two_apart = [[4 * m + b, 4 * m + b + 2] for m in range(cols // 4) for b in range(2)]
    up, down = shifted(up, 1), shifted(down, -1)
    near = exchange(pair, "col", two_apart).sum(0) + up + down
    return exchange(near, "col", far).sum(0)


def swap_cores(value):
    return lax.ppermute(value, "row", [(i, i ^ 1) for i in range(lax.axis_size("row"))])


def dense(density, pattern, branch):
    rows, cols = lax.axis_size("row"), lax.axis_size("col")
    layers = lax.axis_size("depth")
    row, col, layer = lax.axis_index("row"), lax.axis_index("col"), lax.axis_index("depth")
    height, width = density.shape
    sub = width // layers
    core = row % 2
    cores_apart = [[x * 2 + c for x in range(rows // 2)] for c in range(2)]

    row_ids = lax.broadcasted_iota(jnp.int32, pattern.shape, 0) + row * pattern.shape[0]
    col_ids = lax.broadcasted_iota(jnp.int32, pattern.shape, 1) + col * pattern.shape[1]
    tiles = jnp.where(row_ids == col_ids, 1, pattern).T.astype(jnp.float32)
    keep = jnp.repeat(jnp.repeat(tiles, TILE, axis=0), TILE, axis=1)
    keep_part = lax.dynamic_slice_in_dim(keep, layer * sub, sub, 0)

    panel = density.T * keep
    part = lax.dynamic_slice_in_dim(panel, layer * sub, sub, 0)
    for step in range(STEPS):
        mine = panel.T.reshape(height // width, layers, sub, width)
        mine = lax.dynamic_index_in_dim(mine, layer, 1, keepdims=False)
        own = gather(mine, "row", rows // 2, cores_apart)
        other = swap_cores(own)

        def product(left, panel=panel):
            out = jnp.dot(
                left.reshape(-1, width), panel, precision=lax.Precision.HIGH, preferred_element_type=jnp.float32
            )
            return out.reshape(rows // 2, 2, sub, height)

        both = jnp.stack([product(own), product(other)])

        def of_class(k, both=both):
            k = k % 4
            start = ((k // 2) ^ core, 0, k % 2, 0, 0)
            out = lax.dynamic_slice(both, start, (1, rows // 2, 1, sub, height))
            return out.reshape(rows // 2, sub, height)

        squared = sum_along_col([of_class(col + q) for q in range(4)])
        part = keep_part * jnp.where(branch[step] == 1, squared, 2.0 * part - squared)
        panel = gather(part, "depth", layers).reshape(width, height)
    return panel.T


def column_order(keep):
    n = keep.shape[0]
    load = keep.sum(0)
    ids = jnp.arange(n)
    ahead = (load[None, :] > load[:, None]) | ((load[None, :] == load[:, None]) & (ids[None, :] < ids[:, None]))
    rank = ahead.astype(jnp.int32).sum(1)
    place = jnp.where(rank < n // 2, 2 * rank, 2 * (n - 1 - rank) + 1)
    return jnp.where(place[None, :] == ids[:, None], ids[None, :], 0).sum(1)


def slot_list(held, columns, slots):
    n = held.shape[-1]
    ids = jnp.arange(n)
    upto = (ids[:, None] <= ids[None, :]).astype(jnp.float32)
    count = jnp.dot(held.astype(jnp.float32), upto).astype(jnp.int32)
    which = jnp.arange(2)[:, None]
    place = count - 1 + which * count[..., :1, -1:]
    value = 1 + 2 * n * (n * columns[..., None] + ids) + n * which + ids
    hit = (held > 0)[..., None] & (place[..., None] == jnp.arange(2 * slots))
    return jnp.where(hit, value[..., None], 0).sum((-3, -2))


def spot(packed, blocks, in_product):
    at = jnp.maximum(packed - 1, 0)
    at = at >> blocks.bit_length() if in_product else at & (2 * blocks - 1)
    return at >> (blocks.bit_length() - 1), pl.ds(pl.multiple_of((at & (blocks - 1)) * TILE, TILE), TILE)


def pick_kernel(info_ref, from_ref, out_ref, *, slots, blocks):
    for t in range(slots):
        block, lanes = spot(info_ref[t], blocks, False)
        rows = pl.ds(pl.multiple_of(block * LANES, LANES), LANES)
        out_ref[t * LANES : (t + 1) * LANES, :] = jnp.where(info_ref[t] > 0, from_ref[rows, lanes], 0.0)


def place_kernel(info_ref, own_ref, other_ref, out_ref, *, slots, blocks):
    out_ref[...] = jnp.zeros_like(out_ref)
    for base, ref in ((0, own_ref), (slots, other_ref)):
        for t in range(slots):
            block, lanes = spot(info_ref[base + t], blocks, False)

            @pl.when(info_ref[base + t] > 0)
            def _(block=block, lanes=lanes, ref=ref, t=t):
                rows = pl.ds(pl.multiple_of(block * LANES, LANES), LANES)
                out_ref[rows, lanes] = ref[t * LANES : (t + 1) * LANES, :]


def step_kernel(info_ref, own_ref, other_ref, out_ref, x_ref, hi_ref, lo_ref, left_ref, prod_ref,
                *, slots_in, slots_out, blocks):
    share, square = info_ref[0], info_ref[3]
    sharers = TILE // LANES
    x_ref[...] = jnp.zeros_like(x_ref)
    for base, ref in ((4, own_ref), (4 + slots_in, other_ref)):

        def place(t, _, base=base, ref=ref):
            block, lanes = spot(info_ref[base + t], blocks, False)

            @pl.when(info_ref[base + t] > 0)
            def _():
                rows = pl.ds(pl.multiple_of(t * LANES, LANES), LANES)
                for s in range(sharers):
                    at = pl.multiple_of(block * TILE + s * LANES, LANES)
                    x_ref[pl.ds(at, LANES), lanes] = ref[s, rows, :]

            return 0

        lax.fori_loop(0, slots_in, place, 0)

    group = lax.broadcasted_iota(jnp.int32, (x_ref.shape[0], TILE), 1) // LANES
    for j in range(blocks):
        lanes = slice(j * TILE, (j + 1) * TILE)
        x = x_ref[:, lanes]
        hi = x.astype(jnp.bfloat16)
        hi_ref[:, lanes] = hi
        lo_ref[:, lanes] = (x - hi.astype(jnp.float32)).astype(jnp.bfloat16)
        half = slice(j // sharers * TILE, (j // sharers + 1) * TILE)
        turned = pltpu.roll(x, ((j - share) & (sharers - 1)) * LANES, 1)
        left_ref[:, half] = jnp.where(group == j % sharers, turned, left_ref[:, half])
    left = left_ref[...].T
    a_hi = left.astype(jnp.bfloat16)
    a_lo = (left - a_hi.astype(jnp.float32)).astype(jnp.bfloat16)
    wide = 4 * TILE
    for j in range(blocks * TILE // wide):
        lanes = slice(j * wide, (j + 1) * wide)
        b_hi, b_lo = hi_ref[:, lanes], lo_ref[:, lanes]
        prod_ref[:, lanes] = (
            jnp.dot(a_hi, b_hi, preferred_element_type=jnp.float32)
            + jnp.dot(a_hi, b_lo, preferred_element_type=jnp.float32)
            + jnp.dot(a_lo, b_hi, preferred_element_type=jnp.float32)
        )

    sign = jnp.where(square == 1, 1.0, -1.0)
    weight = jnp.where(square == 1, 0.0, -2.0)
    for half in range(2):
        rows = pl.ds(pl.multiple_of(info_ref[1 + half] * LANES, LANES), LANES)
        mine = pl.ds(pl.multiple_of(half * TILE + share * LANES, LANES), LANES)
        prod_ref[rows, :] = prod_ref[rows, :] + weight * x_ref[mine, :]

    first = 4 + 2 * slots_in

    def pick(t, _):
        packed = info_ref[first + t]
        block, lanes = spot(packed, blocks, True)
        rows = pl.ds(pl.multiple_of(block * LANES, LANES), LANES)
        out = pl.ds(pl.multiple_of(t * LANES, LANES), LANES)
        out_ref[out, :] = jnp.where(packed > 0, sign * prod_ref[rows, lanes], 0.0)
        return 0

    lax.fori_loop(0, out_ref.shape[0] // LANES, pick, 0, unroll=8)


def on_core(kernel, shape, scratch=()):
    vmem_spec, smem_spec = pl.BlockSpec(memory_space=pltpu.VMEM), pl.BlockSpec(memory_space=pltpu.SMEM)

    def call(info, *arrays):
        return pl.pallas_call(
            kernel,
            out_shape=jax.ShapeDtypeStruct(shape, jnp.float32),
            in_specs=[smem_spec] + [vmem_spec] * len(arrays),
            out_specs=vmem_spec,
            scratch_shapes=list(scratch),
            compiler_params=pltpu.CompilerParams(vmem_limit_bytes=48 * 1024 * 1024),
        )(info, *arrays)

    return call


def plane_groups():
    rows, layers = lax.axis_size("row"), lax.axis_size("depth")
    return [[(x * 2 + c) * layers + y for x in range(rows // 2) for y in range(layers)] for c in range(2)]


def in_plane(part):
    own = gather(part, ("row", "depth"), TILE // LANES, plane_groups())
    return own, swap_cores(own)


def sparse(own, other, natural, balanced, order, branch):
    rows, cols, layers = lax.axis_size("row"), lax.axis_size("col"), lax.axis_size("depth")
    row, col, layer = lax.axis_index("row"), lax.axis_index("col"), lax.axis_index("depth")
    core, share = row % 2, (row // 2) * layers + layer
    blocks = order.shape[0]
    whole = blocks * TILE
    layouts = [(natural, NATURAL, jnp.arange(blocks))] + [(balanced, BALANCED, order)] * (STEPS - 1)
    layouts = layouts + [layouts[0]]

    def of_plane(packed):
        packed = packed.reshape(cols, 2, -1)
        both = lax.dynamic_index_in_dim(packed, col, 0, keepdims=False)
        return jnp.where(core == 0, both, both[::-1]).reshape(-1)

    def for_planes(packed):
        packed = packed.reshape(cols // 4, 4, 2, -1)
        packed = lax.dynamic_index_in_dim(packed, core, 2, keepdims=False)
        classes = (col % 2, col % 2 + 2, (col + 1) % 4, (col + 3) % 4)
        parts = [lax.dynamic_index_in_dim(packed, k, 1, keepdims=False) for k in classes]
        return jnp.concatenate([v.reshape(-1) for v in parts])

    part = None
    for step in range(STEPS):
        now, slots_in, columns = layouts[step]
        then, slots_out, _ = layouts[step + 1]
        if step > 0:
            own, other = in_plane(part)
        info = jnp.concatenate(
            [
                share[None],
                lax.dynamic_slice_in_dim(columns, 2 * col, 2, 0),
                branch[step][None],
                of_plane(now),
                for_planes(then),
            ]
        ).astype(jnp.int32)
        wide = 2 * TILE
        out = on_core(
            functools.partial(step_kernel, slots_in=slots_in, slots_out=slots_out, blocks=blocks),
            (cols * slots_out * LANES, TILE),
            scratch=(
                pltpu.VMEM((wide, whole), jnp.float32),
                pltpu.VMEM((wide, whole), jnp.bfloat16),
                pltpu.VMEM((wide, whole), jnp.bfloat16),
                pltpu.VMEM((wide, blocks * LANES), jnp.float32),
                pltpu.VMEM((blocks * LANES, whole), jnp.float32),
            ),
        )(info, own, other)
        out = out.reshape(4, cols // 4, slots_out * LANES, TILE)
        part = sum_slots(out[:2], out[2], out[3])

    strips = on_core(
        functools.partial(place_kernel, slots=NATURAL, blocks=blocks), (2 * LANES, whole)
    )(of_plane(natural), part, swap_cores(part))
    sharers, height = TILE // LANES, whole // rows
    cut = strips.reshape(2 * LANES, rows // 2, 2, height)
    cut = lax.dynamic_index_in_dim(cut, core, 2, keepdims=False).transpose(1, 0, 2)
    cut = jnp.broadcast_to(cut[:, None], (rows // 2, layers) + cut.shape[1:]).reshape(sharers, 2 * LANES, height)
    back = exchange(cut, ("row", "depth"), plane_groups())
    back = back.reshape(sharers, 2, LANES, height).transpose(1, 0, 2, 3).reshape(2 * TILE, height)
    return back.T


def local(density, pattern, branch):
    rows, cols, layers = lax.axis_size("row"), lax.axis_size("col"), lax.axis_size("depth")
    row, col, layer = lax.axis_index("row"), lax.axis_index("col"), lax.axis_index("depth")
    height, width = density.shape
    blocks = rows * pattern.shape[0]
    cut = density.T.reshape(2, rows // 2, layers, LANES, height)
    cut = lax.dynamic_index_in_dim(cut, layer, 2, keepdims=False).transpose(1, 0, 2, 3)
    cut = cut.reshape(rows // 2, 2 * LANES, height)
    marks = jnp.zeros((LANES, height), jnp.float32).at[:2, : pattern.shape[0]].set(pattern.T.astype(jnp.float32))
    cut = jnp.concatenate([cut, jnp.broadcast_to(marks[None], (rows // 2,) + marks.shape)], axis=1)
    cut = jnp.broadcast_to(cut[:, None], (rows // 2, 2) + cut.shape[1:]).reshape((rows,) + cut.shape[1:])
    got = exchange(cut, "row")
    strips = got[:, : 2 * LANES].transpose(1, 0, 2).reshape(2 * LANES, rows * height)
    marks = got[:, 2 * LANES : 2 * LANES + 2, : pattern.shape[0]].transpose(1, 0, 2).reshape(2, blocks)

    ids = jnp.arange(blocks)
    sent = jnp.zeros((LANES, TILE), jnp.float32).at[:2, :blocks].set(marks)
    steps = [(r, z, y, (z - r // 2 * layers - y) % cols) for r in range(rows) for z in range(cols) for y in range(layers)]
    ahead = lax.ppermute(
        sent,
        ("row", "col", "depth"),
        [((r * cols + z) * layers + y, (r * cols + to) * layers + y) for r, z, y, to in steps],
    )
    columns = 2 * col + jnp.arange(2)
    held = jnp.where(columns[:, None] == ids, 1, marks.astype(jnp.int32))
    mine = slot_list(held, columns, NATURAL).reshape(2, NATURAL)
    part = on_core(functools.partial(pick_kernel, slots=NATURAL, blocks=blocks), (NATURAL * LANES, TILE))(
        lax.dynamic_index_in_dim(mine, row % 2, 0, keepdims=False), strips
    )
    own, other = in_plane(jnp.concatenate([part, ahead]))
    seen = own[:, NATURAL * LANES : NATURAL * LANES + 2, :blocks].reshape(2 * cols, blocks)
    seen = lax.dynamic_slice_in_dim(jnp.concatenate([seen, seen]), 2 * (cols - col), 2 * cols, 0)
    keep = jnp.where(ids[:, None] == ids[None, :], 1, seen.astype(jnp.int32))
    order = column_order(keep)
    moved = jnp.dot((order[:, None] == ids).astype(jnp.float32), keep.astype(jnp.float32)).astype(jnp.int32)

    def in_pairs(rows_of):
        return rows_of.reshape((cols, 2) + rows_of.shape[1:])

    natural = slot_list(in_pairs(keep), in_pairs(ids), NATURAL)
    balanced = slot_list(in_pairs(moved), in_pairs(order), BALANCED)
    spare = jnp.stack(
        [2 * NATURAL - in_pairs(keep).sum((1, 2)), 2 * BALANCED - in_pairs(moved).sum((1, 2))]
    )
    purified = sparse(own, other, natural, balanced, order, branch)
    return lax.cond(spare.min() >= 0, lambda: purified, lambda: dense(density, pattern, branch))


def solution(mesh):
    in_specs = (P("row", "col"), P("row", "col"), P())
    out_specs = P("row", "col")
    return jax.shard_map(local, mesh=mesh, in_specs=in_specs, out_specs=out_specs, check_vma=False)
```
